256 devices in a mesh: row: 8 (over x, y_hi), col: 32 (over y_lo, z, core).
Axes of the slice: x: 4, y: 4 (y_hi: 2, y_lo: 2; y = y_hi * 2 + y_lo), z: 8, core: 2. Of those that a mesh axis runs over, the one named last changes fastest.
Arguments:
- x_blocks: float32 [8, 128, 128, 128], P('row', 'col'), may hold values from -0.5 to 0.5
- x_rows: int32 [8, 128], P('row', 'col'), may hold values from 0 to 75, as said below
- x_cols: int32 [8, 128], P('row', 'col'), may hold values from 0 to 18, as said below
- y_blocks: float32 [608, 32, 128, 128], P('row', 'col'), may hold values from -6 to 6
- y_cols: int32 [608, 32], P('row', 'col'), may hold values from 0 to 18, as said below
- z_rows: int32 [8, 1280], P('row', 'col'), may hold values from 0 to 75, as said below
- z_cols: int32 [8, 1280], P('row', 'col'), may hold values from 0 to 18, as said below
Outputs:
- z_blocks: float32 [8, 1280, 128, 128], P('row', 'col')
The draws below stay inside these ranges and needn't reach their ends.
Inputs may be any that keep to these rules, and one draw needn't show every extreme that they name: `x_rows`: position of a stored block of X inside its grid cell of 76 block rows; positions may repeat. `x_cols`: position of a stored block of X inside its grid cell of 19 block columns. `y_cols`: position of a stored block of Y inside its column cell of 19 block columns. `z_rows`: every retained position of the product receives at least one product of a stored block of X with a stored block of Y; positions may repeat. `z_cols`: column position of a retained product block inside its cell.
All inputs are finite; a program needn't handle non-finite values.
Results may differ from the reference program's by a relative error of at most 0.0003.
Values sent between devices are 32-bit elements; how exact they have to be, the bound alone decides.
No kernel may reach another device: no remote copies, remote signals or barrier semaphores. Data moves between devices by JAX's collectives and lax.ppermute only.
A program may use at most 128 MiB of HBM per device.

```python
import jax
import jax.numpy as jnp
from jax import lax

BLK = 128
NB = 608
SA = 4
SC = 40
SB = 1
BR = 76
BC = 19
N_ROW = 8
N_COL = 32


def block_pattern(key):
    x_rows = jax.random.randint(jax.random.fold_in(key, 101), (N_ROW, N_COL * SA), 0, BR, dtype=jnp.int32)
    x_cols = jax.random.randint(jax.random.fold_in(key, 102), (N_ROW, N_COL * SA), 0, BC, dtype=jnp.int32)
    y_cols = jax.random.randint(jax.random.fold_in(key, 103), (NB, N_COL * SB), 0, BC, dtype=jnp.int32)
    chosen = jax.random.randint(jax.random.fold_in(key, 104), (N_ROW, N_COL * SC), 0, N_COL * SA, dtype=jnp.int32)
    which = jax.random.randint(jax.random.fold_in(key, 105), (N_ROW, N_COL * SC), 0, SB, dtype=jnp.int32)
    z_rows = jnp.take_along_axis(x_rows, chosen, axis=1)
    picked_cols = jnp.take_along_axis(x_cols, chosen, axis=1)
    inner_index = chosen // SA * BC + picked_cols
    cell_ids = jnp.arange(N_COL * SC, dtype=jnp.int32)[None, :] // SC
    z_cols = y_cols[inner_index, cell_ids * SB + which]
    return (x_rows, x_cols, y_cols, z_rows, z_cols)


def draw_x_rows(key, part):
    shared = block_pattern(key)
    return shared[0]


def draw_x_cols(key, part):
    shared = block_pattern(key)
    return shared[1]


def draw_y_cols(key, part):
    shared = block_pattern(key)
    return shared[2]


def draw_z_rows(key, part):
    shared = block_pattern(key)
    return shared[3]


def draw_z_cols(key, part):
    shared = block_pattern(key)
    return shared[4]


def block_levels(key, shape, shards, least, largest):
    def one(dim, parts):
        steps = jax.random.uniform(jax.random.fold_in(jax.random.fold_in(key, 6), dim), (parts,), jnp.float32, least / len(shards), largest / len(shards))
        return jnp.repeat(jnp.exp(steps), shape[dim] // parts).reshape((-1,) + (1,) * (len(shape) - dim - 1))

    factor_of = one(*shards[0])
    for cut in shards[1:]:
        factor_of = factor_of * one(*cut)
    return factor_of


def normal_values(key, extent, width, reach, cuts=(), held_as=jnp.bfloat16):
    values = jax.random.normal(key, extent, jnp.float32) * width
    if len(cuts) > 0:
        values = block_levels(key, extent, cuts, -0.22, 0.18) * values
    return jnp.clip(values, min=-reach, max=reach).astype(held_as)


def setup_inputs(seed: int = 0) -> dict:
    splits = jax.random.split(jax.random.key(seed), 8)
    x_blocks = normal_values(splits[0], (N_ROW, N_COL * SA, BLK, BLK), BLK ** -0.5, 0.5, ((0, 8), (1, 32)), jnp.float32)
    x_rows = draw_x_rows(jax.random.fold_in(splits[7], 71), 0)
    x_cols = draw_x_cols(jax.random.fold_in(splits[7], 71), 0)
    y_blocks = normal_values(splits[3], (NB, N_COL * SB, BLK, BLK), 1.0, 6.0, ((0, 8), (1, 32)), jnp.float32)
    y_cols = draw_y_cols(jax.random.fold_in(splits[7], 71), 0)
    z_rows = draw_z_rows(jax.random.fold_in(splits[7], 71), 0)
    z_cols = draw_z_cols(jax.random.fold_in(splits[7], 71), 0)
    return dict(x_blocks=x_blocks, x_rows=x_rows, x_cols=x_cols, y_blocks=y_blocks, y_cols=y_cols, z_rows=z_rows, z_cols=z_cols)


def reference(x_blocks, x_rows, x_cols, y_blocks, y_cols, z_rows, z_cols):
    y_grid = y_blocks.reshape(NB, N_COL, SB, BLK, BLK)
    y_where = y_cols.reshape(NB, N_COL, SB)

    def one_panel(panel_index):
        left_blocks = x_blocks[panel_index]
        row_ids = x_rows[panel_index]
        cell_ids = jnp.arange(N_COL * SA, dtype=jnp.int32) // SA
        inner_index = (cell_ids * BC + x_cols[panel_index]).astype(jnp.int32)
        keep_rows = z_rows[panel_index].reshape(N_COL, SC)
        keep_cols = z_cols[panel_index].reshape(N_COL, SC)

        def one_cell(cell_index):
            right_blocks = y_grid[inner_index, cell_index]
            right_cols = y_where[inner_index, cell_index]
            products = jnp.einsum("pxy,ptyz->ptxz", left_blocks, right_blocks, precision=lax.Precision.HIGHEST)
            want_rows = keep_rows[cell_index]
            want_cols = keep_cols[cell_index]
            matches = (want_rows[:, None, None] == row_ids[None, :, None]) & (want_cols[:, None, None] == right_cols[None, :, :])
            return jnp.einsum("spt,ptxz->sxz", matches.astype(jnp.float32), products, precision=lax.Precision.HIGHEST)

        result = lax.map(one_cell, jnp.arange(N_COL, dtype=jnp.int32))
        return result.reshape(N_COL * SC, BLK, BLK)

    return lax.map(one_panel, jnp.arange(N_ROW, dtype=jnp.int32))
```

```python
import functools

import jax
import jax.numpy as jnp
from jax import lax
from jax.experimental import pallas as pl
from jax.experimental.pallas import tpu as pltpu
from jax.sharding import Mesh
from jax.sharding import PartitionSpec as P

LANES = 128
SLOTS = (5, 6, 7, 8, 9, 10, 11, 12, 14, 16)
TOGETHER = 4
HBM = pl.BlockSpec(memory_space=pltpu.HBM)
ANY = pl.BlockSpec(memory_space=pl.ANY)
SMEM = pl.BlockSpec(memory_space=pltpu.SMEM)
VMEM = pl.BlockSpec(memory_space=pltpu.VMEM)


def sheet_kernel(panel, z_rows, z_cols, y_cols, sheet, *, per_cell):
    cols = panel.shape[0]
    got = panel[...].astype(jnp.float32)
    lane = lax.broadcasted_iota(jnp.int32, (LANES, LANES), 1)
    up = lax.broadcasted_iota(jnp.int32, (LANES, LANES), 0)
    cell = lax.broadcasted_iota(jnp.int32, (cols, LANES), 0)
    mine = cell == lax.broadcasted_iota(jnp.int32, (cols, LANES), 1) // per_cell
    lines = []
    for base in (0, per_cell):
        repeated = jnp.dot(
            got,
            (up == base + lane % per_cell).astype(jnp.float32),
            preferred_element_type=jnp.float32,
        )
        lines.append(jnp.sum(jnp.where(mine, repeated, 0.0), axis=0, keepdims=True))
    for v in (z_rows, z_cols, y_cols):
        v = v[...].astype(jnp.float32)
        lines.append(jnp.pad(v, ((0, 0), (0, LANES - v.shape[1]))))
    whole = jnp.concatenate(lines, axis=0).astype(jnp.int32)
    for r in range(sheet.shape[0]):
        sheet[r] = whole


def plan_kernel(
    where, info, plan, pick, spread, *, rows, cell_width, per_cell, group, half, targets, panel_rows
):
    shape = (rows, LANES)
    lane = lax.broadcasted_iota(jnp.int32, shape, 1)
    row = lax.broadcasted_iota(jnp.int32, shape, 0)
    x_row, x_col = info[:, 0, :], info[:, 1, :]
    z_code = info[:, 2, :] * cell_width + info[:, 3, :]
    y_col = info[:, 4, :].astype(jnp.float32)
    owner = lane // group
    inner = (lane // per_cell) % (group // per_cell) * cell_width + x_col
    spread[...] = lax.dot_general(
        y_col,
        (row == owner).astype(jnp.float32),
        (((0,), (0,)), ((), ())),
        preferred_element_type=jnp.float32,
    )
    met = jnp.zeros(shape, jnp.float32)
    for k in range(panel_rows):
        met = jnp.where(inner == k, spread[k : k + 1, :], met)
    code = x_row * cell_width + met.astype(jnp.int32)
    target = jnp.full(shape, -1, jnp.int32)
    first = lane
    for s in reversed(range(targets)):
        wanted = z_code[:, s : s + 1]
        target = jnp.where(code == wanted, s, target)
        first = jnp.where(z_code == wanted, s, first)
    used = target >= 0
    key = jnp.where(used, inner, -1 - lane)
    place = lane % group
    repeat = jnp.zeros(shape, jnp.int32)
    for d in range(1, group):
        same = (pltpu.roll(key, d, 1) == key) & (place >= d)
        repeat = jnp.where(same, d, repeat)
    sent = used & (repeat == 0)
    sent_f = sent.astype(jnp.float32)
    up = lax.broadcasted_iota(jnp.int32, (LANES, LANES), 0)
    across = lax.broadcasted_iota(jnp.int32, (LANES, LANES), 1)
    together = (up // group) == (across // group)
    before = (together & (up < across)).astype(jnp.float32)
    slot = jnp.dot(sent_f, before, preferred_element_type=jnp.float32).astype(jnp.int32)
    count = jnp.dot(sent_f, together.astype(jnp.float32), preferred_element_type=jnp.float32)
    held = slot
    for d in range(1, group):
        held = jnp.where(repeat == d, pltpu.roll(slot, d, 1), held)
    me, side = where[0], where[1]

    own_first = (LANES - group * me) % LANES
    mine = lambda v: pltpu.roll(v, own_first, 1)
    sent_slot, sent_row = mine(jnp.where(sent, slot, -1)), mine(inner)
    send = jnp.zeros(shape, jnp.int32)
    for t in range(group):
        send = jnp.where(lane == sent_slot[:, t : t + 1], sent_row[:, t : t + 1], send)
    plan[0] = send
    plan[1] = mine(count.astype(jnp.int32))

    def own(v):
        return jnp.sum(jnp.where(row == me, v.astype(jnp.float32), 0.0), axis=0, keepdims=True)

    used_f = used.astype(jnp.float32)
    rank = jnp.dot(used_f, (up < across).astype(jnp.float32), preferred_element_type=jnp.float32)
    chosen = (own(rank).astype(jnp.int32) == up) & (own(used_f) > 0.0)
    p = lane[:1]
    cell = p // per_cell
    facts = jnp.concatenate(
        [
            (cell % half * per_cell + p % per_cell).astype(jnp.float32),
            (cell // half == side).astype(jnp.float32),
            owner[:1].astype(jnp.float32),
            own(held),
            own(target),
            own(inner),
            jnp.zeros((2, LANES), jnp.float32),
        ]
    )
    listed = lax.dot_general(
        facts,
        chosen.astype(jnp.float32),
        (((1,), (1,)), ((), ())),
        preferred_element_type=jnp.float32,
    )
    total = jnp.sum(own(used_f), axis=1, keepdims=True)
    plan[2] = jnp.where(
        row == 6, total, jnp.where(row == 7, own(first), listed)
    ).astype(jnp.int32)
    most = jnp.max(jnp.where(owner == row, 0.0, count)).astype(jnp.int32)
    choice = jnp.int32(0)
    for limit in SLOTS[:-1]:
        choice = choice + (most > limit).astype(jnp.int32)
    pick[0] = choice


def pack_kernel(plan, where, y_blocks, out, sem, *, rows):
    me = where[0]
    started = jnp.int32(0)
    for r in range(rows):
        count = jnp.where(me == r, 0, plan[1, r, 0])

        @pl.loop(0, count)
        def _(j):
            pltpu.make_async_copy(y_blocks.at[plan[0, r, j]], out.at[r, j], sem).start()

        started = started + count

    @pl.loop(0, started)
    def _(_):
        pltpu.make_async_copy(y_blocks.at[0], out.at[0, 0], sem).wait()


X_PLACE, X_NEAR, OWNER, SLOT, TARGET, INNER, TOTAL, FIRST = range(8)


def unpack_kernel(plan, where, got, out, sem, *, group):
    me = where[0]

    def start(n, started):
        owner = plan[2, OWNER, n]

        @pl.when(owner != me)
        def _():
            pltpu.make_async_copy(got.at[owner, plan[2, SLOT, n]], out.at[n], sem).start()

        return started + (owner != me).astype(jnp.int32)

    started = lax.fori_loop(0, plan[2, TOTAL, 0], start, jnp.int32(0))

    @pl.loop(0, started)
    def _(_):
        pltpu.make_async_copy(got.at[0, 0], out.at[0], sem).wait()


def product_kernel(
    plan,
    where,
    x_near,
    x_far,
    y_blocks,
    y_lined,
    out,
    x_held,
    y_held,
    sums,
    into,
    x_sem,
    y_sem,
    out_sem,
    *,
    targets,
):
    me = where[0]
    total = plan[2, TOTAL, 0]

    @pl.loop(0, total)
    def _(n):
        place = plan[2, X_PLACE, n]
        near = plan[2, X_NEAR, n] > 0
        here = plan[2, OWNER, n] == me

        @pl.when(near)
        def _():
            pltpu.make_async_copy(x_near.at[place], x_held.at[n], x_sem.at[n]).start()

        @pl.when(jnp.logical_not(near))
        def _():
            pltpu.make_async_copy(x_far.at[place], x_held.at[n], x_sem.at[n]).start()

        @pl.when(here)
        def _():
            pltpu.make_async_copy(
                y_blocks.at[plan[2, INNER, n]], y_held.at[n], y_sem.at[n]
            ).start()

        @pl.when(jnp.logical_not(here))
        def _():
            pltpu.make_async_copy(y_lined.at[n], y_held.at[n], y_sem.at[n]).start()

        into[n] = plan[2, TARGET, n]

    for j in range(TOGETHER - 1):
        into[total + j] = targets
    sums[...] = jnp.zeros_like(sums)
    dot = functools.partial(jnp.dot, preferred_element_type=jnp.float32)

    @pl.loop(0, (total + TOGETHER - 1) // TOGETHER)
    def _(i):
        n = i * TOGETHER
        for j in range(TOGETHER):

            @pl.when(n + j < total)
            def _():
                pltpu.make_async_copy(x_near.at[0], x_held.at[n + j], x_sem.at[n + j]).wait()
                pltpu.make_async_copy(y_lined.at[0], y_held.at[n + j], y_sem.at[n + j]).wait()

        products = []
        for j in range(TOGETHER):
            x, y = x_held[n + j], y_held[n + j]
            x_hi, y_hi = x.astype(jnp.bfloat16), y.astype(jnp.bfloat16)
            x_lo = (x - x_hi.astype(jnp.float32)).astype(jnp.bfloat16)
            y_lo = (y - y_hi.astype(jnp.float32)).astype(jnp.bfloat16)
            products.append(
                dot(
                    jnp.concatenate([x_hi, x_lo, x_hi], axis=1),
                    jnp.concatenate([y_hi, y_hi, y_lo], axis=0),
                )
            )
        for j in range(TOGETHER):
            sums[into[n + j]] += products[j]

    for s in range(targets):
        pltpu.make_async_copy(sums.at[plan[2, FIRST, s]], out.at[s], out_sem).start()
    for s in range(targets):
        pltpu.make_async_copy(sums.at[0], out.at[s], out_sem).wait()


def local(x_blocks, x_rows, x_cols, y_blocks, y_cols, z_rows, z_cols):
    row_axes, col_axes = ("x", "y_hi"), ("y_lo", "z", "core")
    rows, cols = lax.axis_size(row_axes), lax.axis_size(col_axes)
    x_blocks = x_blocks[0]
    y_blocks = y_blocks[:, 0]
    per_cell, edge = x_blocks.shape[0], x_blocks.shape[-1]
    panel_rows = y_blocks.shape[0]
    targets = z_rows.shape[1]
    group = cols * per_cell // rows
    cell_width = panel_rows * rows // cols
    half = cols // 2
    me = lax.axis_index(row_axes)
    where = jnp.stack([me, lax.axis_index("y_lo")]).astype(jnp.int32)
    block = (edge, edge)

    across = lax.ppermute(x_blocks, "y_lo", [(0, 1), (1, 0)])
    x_near = lax.all_gather(x_blocks, ("z", "core"), axis=0, tiled=True)

    own = jnp.pad(jnp.concatenate([x_rows[0], x_cols[0]]), (0, LANES - 2 * per_cell))
    panel = lax.all_to_all(jnp.broadcast_to(own, (cols, 1, LANES)), col_axes, 0, 0, tiled=True)
    panel = panel.reshape(cols, LANES)
    across, panel = lax.optimization_barrier((across, panel))
    x_far = lax.all_gather(across, ("z", "core"), axis=0, tiled=True)
    sheet = pl.pallas_call(
        functools.partial(sheet_kernel, per_cell=per_cell),
        out_shape=jax.ShapeDtypeStruct((rows, 5, LANES), jnp.int32),
        in_specs=[VMEM] * 4,
        out_specs=VMEM,
        compiler_params=pltpu.CompilerParams(vmem_limit_bytes=4 * 2**20),
        name="sheet",
    )(panel, z_rows, z_cols, y_cols.reshape(1, panel_rows))
    info = lax.all_to_all(sheet, row_axes, 0, 0, tiled=True)

    plan, pick = pl.pallas_call(
        functools.partial(
            plan_kernel,
            rows=rows,
            cell_width=cell_width,
            per_cell=per_cell,
            group=group,
            half=half,
            targets=targets,
            panel_rows=panel_rows,
        ),
        out_shape=(
            jax.ShapeDtypeStruct((3, rows, LANES), jnp.int32),
            jax.ShapeDtypeStruct((1,), jnp.int32),
        ),
        in_specs=[SMEM, VMEM],
        out_specs=(VMEM, SMEM),
        scratch_shapes=[pltpu.VMEM((LANES, LANES), jnp.float32)],
        compiler_params=pltpu.CompilerParams(vmem_limit_bytes=4 * 2**20),
        name="plan",
    )(where, info)

    def with_slots(slots):
        def branch(plan, where, y_blocks):
            packed = pl.pallas_call(
                functools.partial(pack_kernel, rows=rows),
                out_shape=jax.ShapeDtypeStruct((rows, slots) + block, jnp.float32),
                in_specs=[SMEM, SMEM, HBM],
                out_specs=VMEM,
                scratch_shapes=[pltpu.SemaphoreType.DMA],
                compiler_params=pltpu.CompilerParams(vmem_limit_bytes=40 * 2**20),
                name="pack",
            )(plan, where, y_blocks)
            got = lax.all_to_all(packed, row_axes, 0, 0, tiled=True)
            return pl.pallas_call(
                functools.partial(unpack_kernel, group=group),
                out_shape=jax.ShapeDtypeStruct((LANES,) + block, jnp.float32),
                in_specs=[SMEM, SMEM, ANY],
                out_specs=HBM,
                scratch_shapes=[pltpu.SemaphoreType.DMA],
                compiler_params=pltpu.CompilerParams(vmem_limit_bytes=4 * 2**20),
                name="unpack",
            )(plan, where, got)

        return branch

    y_lined = lax.switch(pick[0], [with_slots(s) for s in SLOTS], plan, where, y_blocks)

    out = pl.pallas_call(
        functools.partial(product_kernel, targets=targets),
        out_shape=jax.ShapeDtypeStruct((targets,) + block, jnp.float32),
        in_specs=[SMEM, SMEM, HBM, HBM, HBM, HBM],
        out_specs=HBM,
        scratch_shapes=[
            pltpu.VMEM((LANES,) + block, jnp.float32),
            pltpu.VMEM((LANES,) + block, jnp.float32),
            pltpu.VMEM((targets + 1,) + block, jnp.float32),
            pltpu.SMEM((LANES + TOGETHER,), jnp.int32),
            pltpu.SemaphoreType.DMA((LANES,)),
            pltpu.SemaphoreType.DMA((LANES,)),
            pltpu.SemaphoreType.DMA,
        ],
        compiler_params=pltpu.CompilerParams(vmem_limit_bytes=60 * 2**20),
        name="products",
    )(plan, where, x_near, x_far, y_blocks, y_lined)
    return out[None]


def solution(mesh):
    chips = Mesh(mesh.devices.reshape(4, 2, 2, 8, 2), ("x", "y_hi", "y_lo", "z", "core"))
    row, col = ("x", "y_hi"), ("y_lo", "z", "core")
    flat, blocks = P(row, col), P(row, col, None, None)
    return jax.shard_map(
        local,
        mesh=chips,
        in_specs=(blocks, flat, flat, blocks, flat, flat, flat),
        out_specs=blocks,
        check_vma=False,
    )
```

```python
import functools

import jax
import jax.numpy as jnp
from jax import lax
from jax.experimental import pallas as pl
from jax.experimental.pallas import tpu as pltpu
from jax.sharding import Mesh
from jax.sharding import PartitionSpec as P

LANES = 128
SLOTS = (5, 6, 7, 8, 9, 10, 11, 12, 14, 16)
TOGETHER = 4
HBM = pl.BlockSpec(memory_space=pltpu.HBM)
ANY = pl.BlockSpec(memory_space=pl.ANY)
SMEM = pl.BlockSpec(memory_space=pltpu.SMEM)
VMEM = pl.BlockSpec(memory_space=pltpu.VMEM)


def sheet_kernel(panel, rest, sheet, *, per_cell):
    cols = panel.shape[0]
    got = panel[...].astype(jnp.float32)
    lane = lax.broadcasted_iota(jnp.int32, (LANES, LANES), 1)
    up = lax.broadcasted_iota(jnp.int32, (LANES, LANES), 0)
    cell = lax.broadcasted_iota(jnp.int32, (cols, LANES), 0)
    mine = cell == lax.broadcasted_iota(jnp.int32, (cols, LANES), 1) // per_cell
    lines = []
    for base in (0, per_cell):
        repeated = jnp.dot(
            got,
            (up == base + lane % per_cell).astype(jnp.float32),
            preferred_element_type=jnp.float32,
        )
        lines.append(jnp.sum(jnp.where(mine, repeated, 0.0), axis=0, keepdims=True))
    whole = jnp.concatenate([v.astype(jnp.int32) for v in lines] + [rest[...]], axis=0)
    for r in range(sheet.shape[0]):
        sheet[r] = whole


def plan_kernel(
    where, info, plan, pick, spread, *, rows, cell_width, per_cell, group, half, targets, panel_rows
):
    shape = (rows, LANES)
    lane = lax.broadcasted_iota(jnp.int32, shape, 1)
    row = lax.broadcasted_iota(jnp.int32, shape, 0)
    x_row, x_col = info[:, 0, :], info[:, 1, :]
    z_code = info[:, 2, :] * cell_width + info[:, 3, :]
    y_col = info[:, 4, :].astype(jnp.float32)
    owner = lane // group
    inner = (lane // per_cell) % (group // per_cell) * cell_width + x_col
    spread[...] = lax.dot_general(
        y_col,
        (row == owner).astype(jnp.float32),
        (((0,), (0,)), ((), ())),
        preferred_element_type=jnp.float32,
    )
    met = jnp.zeros(shape, jnp.float32)
    for k in range(panel_rows):
        met = jnp.where(inner == k, spread[k : k + 1, :], met)
    code = x_row * cell_width + met.astype(jnp.int32)
    target = jnp.full(shape, -1, jnp.int32)
    first = lane
    for s in reversed(range(targets)):
        wanted = z_code[:, s : s + 1]
        target = jnp.where(code == wanted, s, target)
        first = jnp.where(z_code == wanted, s, first)
    used = target >= 0
    key = jnp.where(used, inner, -1 - lane)
    place = lane % group
    repeat = jnp.zeros(shape, jnp.int32)
    for d in range(1, group):
        same = (pltpu.roll(key, d, 1) == key) & (place >= d)
        repeat = jnp.where(same, d, repeat)
    sent = used & (repeat == 0)
    sent_f = sent.astype(jnp.float32)
    up = lax.broadcasted_iota(jnp.int32, (LANES, LANES), 0)
    across = lax.broadcasted_iota(jnp.int32, (LANES, LANES), 1)
    together = (up // group) == (across // group)
    before = (together & (up < across)).astype(jnp.float32)
    slot = jnp.dot(sent_f, before, preferred_element_type=jnp.float32).astype(jnp.int32)
    count = jnp.dot(sent_f, together.astype(jnp.float32), preferred_element_type=jnp.float32)
    held = slot
    for d in range(1, group):
        held = jnp.where(repeat == d, pltpu.roll(slot, d, 1), held)
    me, side = where[0], where[1]

    own_first = (LANES - group * me) % LANES
    mine = lambda v: pltpu.roll(v, own_first, 1)
    sent_slot, sent_row = mine(jnp.where(sent, slot, -1)), mine(inner)
    send = jnp.zeros(shape, jnp.int32)
    for t in range(group):
        send = jnp.where(lane == sent_slot[:, t : t + 1], sent_row[:, t : t + 1], send)
    plan[0] = send
    plan[1] = mine(count.astype(jnp.int32))

    def own(v):
        return jnp.sum(jnp.where(row == me, v.astype(jnp.float32), 0.0), axis=0, keepdims=True)

    used_f = used.astype(jnp.float32)
    rank = jnp.dot(used_f, (up < across).astype(jnp.float32), preferred_element_type=jnp.float32)
    chosen = (own(rank).astype(jnp.int32) == up) & (own(used_f) > 0.0)
    p = lane[:1]
    cell = p // per_cell
    facts = jnp.concatenate(
        [
            (cell % half * per_cell + p % per_cell).astype(jnp.float32),
            (cell // half == side).astype(jnp.float32),
            owner[:1].astype(jnp.float32),
            own(held),
            own(target),
            own(inner),
            jnp.zeros((2, LANES), jnp.float32),
        ]
    )
    listed = lax.dot_general(
        facts,
        chosen.astype(jnp.float32),
        (((1,), (1,)), ((), ())),
        preferred_element_type=jnp.float32,
    )
    total = jnp.sum(own(used_f), axis=1, keepdims=True)
    plan[2] = jnp.where(
        row == 6, total, jnp.where(row == 7, own(first), listed)
    ).astype(jnp.int32)
    most = jnp.max(jnp.where(owner == row, 0.0, count)).astype(jnp.int32)
    choice = jnp.int32(0)
    for limit in SLOTS[:-1]:
        choice = choice + (most > limit).astype(jnp.int32)
    pick[0] = choice


def pack_kernel(plan, where, y_blocks, out, sem, *, rows):
    me = where[0]
    started = jnp.int32(0)
    for r in range(rows):
        count = jnp.where(me == r, 0, plan[1, r, 0])

        @pl.loop(0, count)
        def _(j):
            pltpu.make_async_copy(y_blocks.at[plan[0, r, j]], out.at[r, j], sem).start()

        started = started + count

    @pl.loop(0, started)
    def _(_):
        pltpu.make_async_copy(y_blocks.at[0], out.at[0, 0], sem).wait()


X_PLACE, X_NEAR, OWNER, SLOT, TARGET, INNER, TOTAL, FIRST = range(8)


def unpack_kernel(plan, where, got, out, sem, *, group):
    me = where[0]

    def start(n, started):
        owner = plan[2, OWNER, n]

        @pl.when(owner != me)
        def _():
            pltpu.make_async_copy(got.at[owner, plan[2, SLOT, n]], out.at[n], sem).start()

        return started + (owner != me).astype(jnp.int32)

    started = lax.fori_loop(0, plan[2, TOTAL, 0], start, jnp.int32(0))

    @pl.loop(0, started)
    def _(_):
        pltpu.make_async_copy(got.at[0, 0], out.at[0], sem).wait()


def product_kernel(
    plan,
    where,
    x_near,
    x_far,
    y_blocks,
    y_lined,
    out,
    x_held,
    y_held,
    sums,
    into,
    x_sem,
    y_sem,
    out_sem,
    *,
    targets,
):
    me = where[0]
    total = plan[2, TOTAL, 0]

    @pl.loop(0, total)
    def _(n):
        place = plan[2, X_PLACE, n]
        near = plan[2, X_NEAR, n] > 0
        here = plan[2, OWNER, n] == me

        @pl.when(near)
        def _():
            pltpu.make_async_copy(x_near.at[place], x_held.at[n], x_sem.at[n]).start()

        @pl.when(jnp.logical_not(near))
        def _():
            pltpu.make_async_copy(x_far.at[place], x_held.at[n], x_sem.at[n]).start()

        @pl.when(here)
        def _():
            pltpu.make_async_copy(
                y_blocks.at[plan[2, INNER, n]], y_held.at[n], y_sem.at[n]
            ).start()

        @pl.when(jnp.logical_not(here))
        def _():
            pltpu.make_async_copy(y_lined.at[n], y_held.at[n], y_sem.at[n]).start()

        into[n] = plan[2, TARGET, n]

    for j in range(TOGETHER - 1):
        into[total + j] = targets
    sums[...] = jnp.zeros_like(sums)
    dot = functools.partial(jnp.dot, preferred_element_type=jnp.float32)

    @pl.loop(0, (total + TOGETHER - 1) // TOGETHER)
    def _(i):
        n = i * TOGETHER
        for j in range(TOGETHER):

            @pl.when(n + j < total)
            def _():
                pltpu.make_async_copy(x_near.at[0], x_held.at[n + j], x_sem.at[n + j]).wait()
                pltpu.make_async_copy(y_lined.at[0], y_held.at[n + j], y_sem.at[n + j]).wait()

        products = []
        for j in range(TOGETHER):
            x, y = x_held[n + j], y_held[n + j]
            x_hi, y_hi = x.astype(jnp.bfloat16), y.astype(jnp.bfloat16)
            x_lo = (x - x_hi.astype(jnp.float32)).astype(jnp.bfloat16)
            y_lo = (y - y_hi.astype(jnp.float32)).astype(jnp.bfloat16)
            products.append(
                dot(
                    jnp.concatenate([x_hi, x_lo, x_hi], axis=1),
                    jnp.concatenate([y_hi, y_hi, y_lo], axis=0),
                )
            )
        for j in range(TOGETHER):
            sums[into[n + j]] += products[j]

    for s in range(targets):
        pltpu.make_async_copy(sums.at[plan[2, FIRST, s]], out.at[s], out_sem).start()
    for s in range(targets):
        pltpu.make_async_copy(sums.at[0], out.at[s], out_sem).wait()


def local(x_blocks, x_rows, x_cols, y_blocks, y_cols, z_rows, z_cols):
    row_axes, col_axes = ("x", "y_hi"), ("y_lo", "z", "core")
    rows, cols = lax.axis_size(row_axes), lax.axis_size(col_axes)
    x_blocks = x_blocks[0]
    y_blocks = y_blocks[:, 0]
    per_cell, edge = x_blocks.shape[0], x_blocks.shape[-1]
    panel_rows = y_blocks.shape[0]
    targets = z_rows.shape[1]
    group = cols * per_cell // rows
    cell_width = panel_rows * rows // cols
    half = cols // 2
    me = lax.axis_index(row_axes)
    where = jnp.stack([me, lax.axis_index("y_lo")]).astype(jnp.int32)
    block = (edge, edge)

    own = jnp.pad(jnp.concatenate([x_rows[0], x_cols[0]]), (0, LANES - 2 * per_cell))
    own = jnp.broadcast_to(own, (cols, 1, LANES))
    rest = jnp.stack(
        [jnp.pad(v, (0, LANES - v.shape[0])) for v in (z_rows[0], z_cols[0], y_cols[:, 0])]
    )
    own, x_blocks = lax.optimization_barrier((own, x_blocks))
    panel = lax.all_to_all(own, col_axes, 0, 0, tiled=True).reshape(cols, LANES)
    panel, rest, where = lax.optimization_barrier((panel, rest, where))

    across = lax.ppermute(x_blocks, "y_lo", [(0, 1), (1, 0)])
    x_near = lax.all_gather(x_blocks, ("z", "core"), axis=0, tiled=True)

    sheet = pl.pallas_call(
        functools.partial(sheet_kernel, per_cell=per_cell),
        out_shape=jax.ShapeDtypeStruct((rows, 5, LANES), jnp.int32),
        in_specs=[VMEM] * 2,
        out_specs=VMEM,
        compiler_params=pltpu.CompilerParams(vmem_limit_bytes=4 * 2**20),
        name="sheet",
    )(panel, rest)
    info = lax.all_to_all(sheet, row_axes, 0, 0, tiled=True)
    info, across = lax.optimization_barrier((info, across))
    x_far = lax.all_gather(across, ("z", "core"), axis=0, tiled=True)

    plan, pick = pl.pallas_call(
        functools.partial(
            plan_kernel,
            rows=rows,
            cell_width=cell_width,
            per_cell=per_cell,
            group=group,
            half=half,
            targets=targets,
            panel_rows=panel_rows,
        ),
        out_shape=(
            jax.ShapeDtypeStruct((3, rows, LANES), jnp.int32),
            jax.ShapeDtypeStruct((1,), jnp.int32),
        ),
        in_specs=[SMEM, VMEM],
        out_specs=(VMEM, SMEM),
        scratch_shapes=[pltpu.VMEM((LANES, LANES), jnp.float32)],
        compiler_params=pltpu.CompilerParams(vmem_limit_bytes=4 * 2**20),
        name="plan",
    )(where, info)

    def with_slots(slots):
        def branch(plan, where, y_blocks):
            packed = pl.pallas_call(
                functools.partial(pack_kernel, rows=rows),
                out_shape=jax.ShapeDtypeStruct((rows, slots) + block, jnp.float32),
                in_specs=[SMEM, SMEM, HBM],
                out_specs=VMEM,
                scratch_shapes=[pltpu.SemaphoreType.DMA],
                compiler_params=pltpu.CompilerParams(vmem_limit_bytes=40 * 2**20),
                name="pack",
            )(plan, where, y_blocks)
            got = lax.all_to_all(packed, row_axes, 0, 0, tiled=True)
            return pl.pallas_call(
                functools.partial(unpack_kernel, group=group),
                out_shape=jax.ShapeDtypeStruct((LANES,) + block, jnp.float32),
                in_specs=[SMEM, SMEM, ANY],
                out_specs=HBM,
                scratch_shapes=[pltpu.SemaphoreType.DMA],
                compiler_params=pltpu.CompilerParams(vmem_limit_bytes=4 * 2**20),
                name="unpack",
            )(plan, where, got)

        return branch

    y_lined = lax.switch(pick[0], [with_slots(s) for s in SLOTS], plan, where, y_blocks)

    out = pl.pallas_call(
        functools.partial(product_kernel, targets=targets),
        out_shape=jax.ShapeDtypeStruct((targets,) + block, jnp.float32),
        in_specs=[SMEM, SMEM, HBM, HBM, HBM, HBM],
        out_specs=HBM,
        scratch_shapes=[
            pltpu.VMEM((LANES,) + block, jnp.float32),
            pltpu.VMEM((LANES,) + block, jnp.float32),
            pltpu.VMEM((targets + 1,) + block, jnp.float32),
            pltpu.SMEM((LANES + TOGETHER,), jnp.int32),
            pltpu.SemaphoreType.DMA((LANES,)),
            pltpu.SemaphoreType.DMA((LANES,)),
            pltpu.SemaphoreType.DMA,
        ],
        compiler_params=pltpu.CompilerParams(vmem_limit_bytes=60 * 2**20),
        name="products",
    )(plan, where, x_near, x_far, y_blocks, y_lined)
    return out[None]


def solution(mesh):
    chips = Mesh(mesh.devices.reshape(4, 2, 2, 8, 2), ("x", "y_hi", "y_lo", "z", "core"))
    row, col = ("x", "y_hi"), ("y_lo", "z", "core")
    flat, blocks = P(row, col), P(row, col, None, None)
    return jax.shard_map(
        local,
        mesh=chips,
        in_specs=(blocks, flat, flat, blocks, flat, flat, flat),
        out_specs=blocks,
        check_vma=False,
    )
```

```python
import functools

import jax
import jax.numpy as jnp
from jax import lax
from jax.experimental import pallas as pl
from jax.experimental.pallas import tpu as pltpu
from jax.sharding import Mesh
from jax.sharding import PartitionSpec as P

LANES = 128
SLOTS = (5, 6, 7, 8, 9, 10, 11, 12, 14, 16)
TOGETHER = 8
HBM = pl.BlockSpec(memory_space=pltpu.HBM)
ANY = pl.BlockSpec(memory_space=pl.ANY)
SMEM = pl.BlockSpec(memory_space=pltpu.SMEM)
VMEM = pl.BlockSpec(memory_space=pltpu.VMEM)


def sheet_kernel(panel, rest, sheet, *, per_cell):
    cols = panel.shape[0]
    got = panel[...].astype(jnp.float32)
    lane = lax.broadcasted_iota(jnp.int32, (LANES, LANES), 1)
    up = lax.broadcasted_iota(jnp.int32, (LANES, LANES), 0)
    cell = lax.broadcasted_iota(jnp.int32, (cols, LANES), 0)
    mine = cell == lax.broadcasted_iota(jnp.int32, (cols, LANES), 1) // per_cell
    lines = []
    for base in (0, per_cell):
        repeated = jnp.dot(
            got,
            (up == base + lane % per_cell).astype(jnp.float32),
            preferred_element_type=jnp.float32,
        )
        lines.append(jnp.sum(jnp.where(mine, repeated, 0.0), axis=0, keepdims=True))
    whole = jnp.concatenate([v.astype(jnp.int32) for v in lines] + [rest[...]], axis=0)
    for r in range(sheet.shape[0]):
        sheet[r] = whole


def plan_kernel(
    where, info, plan, pick, spread, *, rows, cell_width, per_cell, group, half, targets, panel_rows
):
    shape = (rows, LANES)
    lane = lax.broadcasted_iota(jnp.int32, shape, 1)
    row = lax.broadcasted_iota(jnp.int32, shape, 0)
    x_row, x_col = info[:, 0, :], info[:, 1, :]
    z_code = info[:, 2, :] * cell_width + info[:, 3, :]
    y_col = info[:, 4, :].astype(jnp.float32)
    owner = lane // group
    inner = (lane // per_cell) % (group // per_cell) * cell_width + x_col
    spread[...] = lax.dot_general(
        y_col,
        (row == owner).astype(jnp.float32),
        (((0,), (0,)), ((), ())),
        preferred_element_type=jnp.float32,
    )
    met = jnp.zeros(shape, jnp.float32)
    for k in range(panel_rows):
        met = jnp.where(inner == k, spread[k : k + 1, :], met)
    code = x_row * cell_width + met.astype(jnp.int32)
    target = jnp.full(shape, -1, jnp.int32)
    first = lane
    for s in reversed(range(targets)):
        wanted = z_code[:, s : s + 1]
        target = jnp.where(code == wanted, s, target)
        first = jnp.where(z_code == wanted, s, first)
    used = target >= 0
    key = jnp.where(used, inner, -1 - lane)
    place = lane % group
    repeat = jnp.zeros(shape, jnp.int32)
    for d in range(1, group):
        same = (pltpu.roll(key, d, 1) == key) & (place >= d)
        repeat = jnp.where(same, d, repeat)
    sent = used & (repeat == 0)
    sent_f = sent.astype(jnp.float32)
    up = lax.broadcasted_iota(jnp.int32, (LANES, LANES), 0)
    across = lax.broadcasted_iota(jnp.int32, (LANES, LANES), 1)
    together = (up // group) == (across // group)
    before = (together & (up < across)).astype(jnp.float32)
    slot = jnp.dot(sent_f, before, preferred_element_type=jnp.float32).astype(jnp.int32)
    count = jnp.dot(sent_f, together.astype(jnp.float32), preferred_element_type=jnp.float32)
    held = slot
    for d in range(1, group):
        held = jnp.where(repeat == d, pltpu.roll(slot, d, 1), held)
    me, side = where[0], where[1]

    own_first = (LANES - group * me) % LANES
    mine = lambda v: pltpu.roll(v, own_first, 1)
    sent_slot, sent_row = mine(jnp.where(sent, slot, -1)), mine(inner)
    send = jnp.zeros(shape, jnp.int32)
    for t in range(group):
        send = jnp.where(lane == sent_slot[:, t : t + 1], sent_row[:, t : t + 1], send)
    plan[0] = send
    plan[1] = mine(count.astype(jnp.int32))

    def own(v):
        return jnp.sum(jnp.where(row == me, v.astype(jnp.float32), 0.0), axis=0, keepdims=True)

    used_f = used.astype(jnp.float32)
    rank = jnp.dot(used_f, (up < across).astype(jnp.float32), preferred_element_type=jnp.float32)
    chosen = (own(rank).astype(jnp.int32) == up) & (own(used_f) > 0.0)
    p = lane[:1]
    cell = p // per_cell
    facts = jnp.concatenate(
        [
            (cell % half * per_cell + p % per_cell).astype(jnp.float32),
            (cell // half == side).astype(jnp.float32),
            owner[:1].astype(jnp.float32),
            own(held),
            own(target),
            own(inner),
            jnp.zeros((2, LANES), jnp.float32),
        ]
    )
    listed = lax.dot_general(
        facts,
        chosen.astype(jnp.float32),
        (((1,), (1,)), ((), ())),
        preferred_element_type=jnp.float32,
    )
    total = jnp.sum(own(used_f), axis=1, keepdims=True)
    plan[2] = jnp.where(
        row == 6, total, jnp.where(row == 7, own(first), listed)
    ).astype(jnp.int32)
    most = jnp.max(jnp.where(owner == row, 0.0, count)).astype(jnp.int32)
    choice = jnp.int32(0)
    for limit in SLOTS[:-1]:
        choice = choice + (most > limit).astype(jnp.int32)
    pick[0] = choice


def pack_kernel(plan, where, y_blocks, out, sem, *, rows):
    me = where[0]
    started = jnp.int32(0)
    for r in range(rows):
        count = jnp.where(me == r, 0, plan[1, r, 0])

        @pl.loop(0, count)
        def _(j):
            pltpu.make_async_copy(y_blocks.at[plan[0, r, j]], out.at[r, j], sem).start()

        started = started + count

    @pl.loop(0, started)
    def _(_):
        pltpu.make_async_copy(y_blocks.at[0], out.at[0, 0], sem).wait()


X_PLACE, X_NEAR, OWNER, SLOT, TARGET, INNER, TOTAL, FIRST = range(8)


def nothing_kernel(*out):
    pass


def product_kernel(plan, where, pick, x_near, x_far, y_blocks, *refs, targets):
    got, (out, x_held, y_held, sums, into, in_sem, out_sem) = refs[:-7], refs[-7:]
    me = where[0]
    total = plan[2, TOTAL, 0]

    for i, brought in enumerate(got):

        @pl.when(pick[0] == i)
        def _():
            @pl.loop(0, total)
            def _(n):
                place, owner = plan[2, X_PLACE, n], plan[2, OWNER, n]
                near, here = plan[2, X_NEAR, n] > 0, owner == me
                sem = in_sem.at[n // TOGETHER]

                @pl.when(near)
                def _():
                    pltpu.make_async_copy(x_near.at[place], x_held.at[n], sem).start()

                @pl.when(jnp.logical_not(near))
                def _():
                    pltpu.make_async_copy(x_far.at[place], x_held.at[n], sem).start()

                @pl.when(here)
                def _():
                    pltpu.make_async_copy(
                        y_blocks.at[plan[2, INNER, n]], y_held.at[n], sem
                    ).start()

                @pl.when(jnp.logical_not(here))
                def _():
                    pltpu.make_async_copy(
                        brought.at[owner, plan[2, SLOT, n]], y_held.at[n], sem
                    ).start()

                into[n] = plan[2, TARGET, n]

    for j in range(TOGETHER - 1):
        into[total + j] = targets
    sums[...] = jnp.zeros_like(sums)
    dot = functools.partial(jnp.dot, preferred_element_type=jnp.float32)

    @pl.loop(0, (total + TOGETHER - 1) // TOGETHER)
    def _(i):
        n = i * TOGETHER
        for j in range(TOGETHER):

            @pl.when(n + j < total)
            def _():
                pltpu.make_async_copy(x_near.at[0], x_held.at[n + j], in_sem.at[i]).wait()
                pltpu.make_async_copy(y_blocks.at[0], y_held.at[n + j], in_sem.at[i]).wait()

        products = []
        for j in range(TOGETHER):
            x, y = x_held[n + j], y_held[n + j]
            x_hi, y_hi = x.astype(jnp.bfloat16), y.astype(jnp.bfloat16)
            x_lo = (x - x_hi.astype(jnp.float32)).astype(jnp.bfloat16)
            y_lo = (y - y_hi.astype(jnp.float32)).astype(jnp.bfloat16)
            products.append(
                dot(
                    jnp.concatenate([x_hi, x_lo, x_hi], axis=1),
                    jnp.concatenate([y_hi, y_hi, y_lo], axis=0),
                )
            )
        for j in range(TOGETHER):
            sums[into[n + j]] += products[j]

    for s in range(targets):
        pltpu.make_async_copy(sums.at[plan[2, FIRST, s]], out.at[s], out_sem).start()
    for s in range(targets):
        pltpu.make_async_copy(sums.at[0], out.at[s], out_sem).wait()


def local(x_blocks, x_rows, x_cols, y_blocks, y_cols, z_rows, z_cols):
    row_axes, col_axes = ("x", "y_hi"), ("y_lo", "z", "core")
    rows, cols = lax.axis_size(row_axes), lax.axis_size(col_axes)
    x_blocks = x_blocks[0]
    y_blocks = y_blocks[:, 0]
    per_cell, edge = x_blocks.shape[0], x_blocks.shape[-1]
    panel_rows = y_blocks.shape[0]
    targets = z_rows.shape[1]
    group = cols * per_cell // rows
    cell_width = panel_rows * rows // cols
    half = cols // 2
    me = lax.axis_index(row_axes)
    where = jnp.stack([me, lax.axis_index("y_lo")]).astype(jnp.int32)
    block = (edge, edge)

    own = jnp.pad(jnp.concatenate([x_rows[0], x_cols[0]]), (0, LANES - 2 * per_cell))
    own = jnp.broadcast_to(own, (cols, 1, LANES))
    rest = jnp.stack(
        [jnp.pad(v, (0, LANES - v.shape[0])) for v in (z_rows[0], z_cols[0], y_cols[:, 0])]
    )
    own, x_blocks = lax.optimization_barrier((own, x_blocks))
    panel = lax.all_to_all(own, col_axes, 0, 0, tiled=True).reshape(cols, LANES)
    panel, rest, where = lax.optimization_barrier((panel, rest, where))

    across = lax.ppermute(x_blocks, "y_lo", [(0, 1), (1, 0)])
    x_near = lax.all_gather(x_blocks, ("z", "core"), axis=0, tiled=True)

    sheet = pl.pallas_call(
        functools.partial(sheet_kernel, per_cell=per_cell),
        out_shape=jax.ShapeDtypeStruct((rows, 5, LANES), jnp.int32),
        in_specs=[VMEM] * 2,
        out_specs=VMEM,
        compiler_params=pltpu.CompilerParams(vmem_limit_bytes=4 * 2**20),
        name="sheet",
    )(panel, rest)
    info = lax.all_to_all(sheet, row_axes, 0, 0, tiled=True)
    info, across = lax.optimization_barrier((info, across))
    x_far = lax.all_gather(across, ("z", "core"), axis=0, tiled=True)

    plan, pick = pl.pallas_call(
        functools.partial(
            plan_kernel,
            rows=rows,
            cell_width=cell_width,
            per_cell=per_cell,
            group=group,
            half=half,
            targets=targets,
            panel_rows=panel_rows,
        ),
        out_shape=(
            jax.ShapeDtypeStruct((3, rows, LANES), jnp.int32),
            jax.ShapeDtypeStruct((1,), jnp.int32),
        ),
        in_specs=[SMEM, VMEM],
        out_specs=(VMEM, SMEM),
        scratch_shapes=[pltpu.VMEM((LANES, LANES), jnp.float32)],
        compiler_params=pltpu.CompilerParams(vmem_limit_bytes=4 * 2**20),
        name="plan",
    )(where, info)

    def room(slots):
        return jax.ShapeDtypeStruct((rows, slots) + block, jnp.float32)

    def with_slots(slots):
        def branch(plan, where, y_blocks):
            packed = pl.pallas_call(
                functools.partial(pack_kernel, rows=rows),
                out_shape=room(slots),
                in_specs=[SMEM, SMEM, HBM],
                out_specs=VMEM,
                scratch_shapes=[pltpu.SemaphoreType.DMA],
                compiler_params=pltpu.CompilerParams(vmem_limit_bytes=40 * 2**20),
                name="pack",
            )(plan, where, y_blocks)
            others = [s for s in SLOTS if s != slots]
            unused = pl.pallas_call(
                nothing_kernel,
                out_shape=[room(s) for s in others],
                out_specs=[HBM] * len(others),
                name="unused",
            )()
            packed, unused = lax.optimization_barrier((packed, unused))
            unused = dict(zip(others, unused, strict=True))
            got = lax.all_to_all(packed, row_axes, 0, 0, tiled=True)
            return [got if s == slots else unused[s] for s in SLOTS]

        return branch

    got = lax.switch(pick[0], [with_slots(s) for s in SLOTS], plan, where, y_blocks)

    out = pl.pallas_call(
        functools.partial(product_kernel, targets=targets),
        out_shape=jax.ShapeDtypeStruct((targets,) + block, jnp.float32),
        in_specs=[SMEM] * 3 + [HBM] * (3 + len(SLOTS)),
        out_specs=HBM,
        scratch_shapes=[
            pltpu.VMEM((LANES,) + block, jnp.float32),
            pltpu.VMEM((LANES,) + block, jnp.float32),
            pltpu.VMEM((targets + 1,) + block, jnp.float32),
            pltpu.SMEM((LANES + TOGETHER,), jnp.int32),
            pltpu.SemaphoreType.DMA((LANES // TOGETHER,)),
            pltpu.SemaphoreType.DMA,
        ],
        compiler_params=pltpu.CompilerParams(vmem_limit_bytes=60 * 2**20),
        name="products",
    )(plan, where, pick, x_near, x_far, y_blocks, *got)
    return out[None]


def solution(mesh):
    chips = Mesh(mesh.devices.reshape(4, 2, 2, 8, 2), ("x", "y_hi", "y_lo", "z", "core"))
    row, col = ("x", "y_hi"), ("y_lo", "z", "core")
    flat, blocks = P(row, col), P(row, col, None, None)
    return jax.shard_map(
        local,
        mesh=chips,
        in_specs=(blocks, flat, flat, blocks, flat, flat, flat),
        out_specs=blocks,
        check_vma=False,
    )
```

```python
import functools

import jax
import jax.numpy as jnp
from jax import lax
from jax.experimental import pallas as pl
from jax.experimental.pallas import tpu as pltpu
from jax.sharding import Mesh
from jax.sharding import PartitionSpec as P

LANES = 128
SLOTS = (5, 6, 7, 8, 9, 10, 11, 12, 14, 16)
TOGETHER = 8
HBM = pl.BlockSpec(memory_space=pltpu.HBM)
ANY = pl.BlockSpec(memory_space=pl.ANY)
SMEM = pl.BlockSpec(memory_space=pltpu.SMEM)
VMEM = pl.BlockSpec(memory_space=pltpu.VMEM)


X_PLACE, X_NEAR, OWNER, SLOT, TARGET, INNER, TOTAL, FIRST = range(8)
ME, PICK = 126, 127


def sheet_kernel(panel, rest, sheet, *, per_cell):
    cols = panel.shape[0]
    got = panel[...].astype(jnp.float32)
    lane = lax.broadcasted_iota(jnp.int32, (LANES, LANES), 1)
    up = lax.broadcasted_iota(jnp.int32, (LANES, LANES), 0)
    cell = lax.broadcasted_iota(jnp.int32, (cols, LANES), 0)
    mine = cell == lax.broadcasted_iota(jnp.int32, (cols, LANES), 1) // per_cell
    lines = []
    for base in (0, per_cell):
        repeated = jnp.dot(
            got,
            (up == base + lane % per_cell).astype(jnp.float32),
            preferred_element_type=jnp.float32,
        )
        lines.append(jnp.sum(jnp.where(mine, repeated, 0.0), axis=0, keepdims=True))
    whole = jnp.concatenate([v.astype(jnp.int32) for v in lines] + [rest[...]], axis=0)
    for r in range(sheet.shape[0]):
        sheet[r] = whole


def plan_kernel(
    info, plan, pick, spread, *, rows, cell_width, per_cell, group, half, targets, panel_rows
):
    shape = (rows, LANES)
    lane = lax.broadcasted_iota(jnp.int32, shape, 1)
    row = lax.broadcasted_iota(jnp.int32, shape, 0)
    x_row, x_col = info[:, 0, :], info[:, 1, :]
    z_code = info[:, 2, :] * cell_width + info[:, 3, :]
    y_col = info[:, 4, :].astype(jnp.float32)
    owner = lane // group
    inner = (lane // per_cell) % (group // per_cell) * cell_width + x_col
    spread[...] = lax.dot_general(
        y_col,
        (row == owner).astype(jnp.float32),
        (((0,), (0,)), ((), ())),
        preferred_element_type=jnp.float32,
    )
    met = jnp.zeros(shape, jnp.float32)
    for k in range(panel_rows):
        met = jnp.where(inner == k, spread[k : k + 1, :], met)
    code = x_row * cell_width + met.astype(jnp.int32)
    target = jnp.full(shape, -1, jnp.int32)
    first = lane
    for s in reversed(range(targets)):
        wanted = z_code[:, s : s + 1]
        target = jnp.where(code == wanted, s, target)
        first = jnp.where(z_code == wanted, s, first)
    used = target >= 0
    key = jnp.where(used, inner, -1 - lane)
    place = lane % group
    repeat = jnp.zeros(shape, jnp.int32)
    for d in range(1, group):
        same = (pltpu.roll(key, d, 1) == key) & (place >= d)
        repeat = jnp.where(same, d, repeat)
    sent = used & (repeat == 0)
    sent_f = sent.astype(jnp.float32)
    up = lax.broadcasted_iota(jnp.int32, (LANES, LANES), 0)
    across = lax.broadcasted_iota(jnp.int32, (LANES, LANES), 1)
    together = (up // group) == (across // group)
    before = (together & (up < across)).astype(jnp.float32)
    slot = jnp.dot(sent_f, before, preferred_element_type=jnp.float32).astype(jnp.int32)
    count = jnp.dot(sent_f, together.astype(jnp.float32), preferred_element_type=jnp.float32)
    held = slot
    for d in range(1, group):
        held = jnp.where(repeat == d, pltpu.roll(slot, d, 1), held)
    me = lax.axis_index("x") * lax.axis_size("y_hi") + lax.axis_index("y_hi")
    side = lax.axis_index("y_lo")

    own_first = (LANES - group * me) % LANES
    mine = lambda v: pltpu.roll(v, own_first, 1)
    sent_slot, sent_row = mine(jnp.where(sent, slot, -1)), mine(inner)
    blocks = jnp.zeros(shape, jnp.int32)
    for t in range(group):
        blocks = jnp.where(lane == sent_slot[:, t : t + 1], sent_row[:, t : t + 1], blocks)
    plan[0] = blocks
    plan[1] = jnp.where(lane == ME, me, mine(count.astype(jnp.int32)))

    def own(v):
        return jnp.sum(jnp.where(row == me, v.astype(jnp.float32), 0.0), axis=0, keepdims=True)

    used_f = used.astype(jnp.float32)
    rank = jnp.dot(used_f, (up < across).astype(jnp.float32), preferred_element_type=jnp.float32)
    chosen = (own(rank).astype(jnp.int32) == up) & (own(used_f) > 0.0)
    p = lane[:1]
    cell = p // per_cell
    facts = jnp.concatenate(
        [
            (cell % half * per_cell + p % per_cell).astype(jnp.float32),
            (cell // half == side).astype(jnp.float32),
            owner[:1].astype(jnp.float32),
            own(held),
            own(target),
            own(inner),
            jnp.zeros((2, LANES), jnp.float32),
        ]
    )
    listed = lax.dot_general(
        facts,
        chosen.astype(jnp.float32),
        (((1,), (1,)), ((), ())),
        preferred_element_type=jnp.float32,
    )
    total = jnp.sum(own(used_f), axis=1, keepdims=True)
    most = jnp.max(jnp.where(owner == row, 0.0, count)).astype(jnp.int32)
    choice = jnp.int32(0)
    for limit in SLOTS[:-1]:
        choice = choice + (most > limit).astype(jnp.int32)
    pick[0] = choice
    scalars = jnp.where(
        lane == ME, me.astype(jnp.float32), jnp.where(lane == PICK, choice.astype(jnp.float32), total)
    )
    plan[2] = jnp.where(
        row == TOTAL, scalars, jnp.where(row == FIRST, own(first), listed)
    ).astype(jnp.int32)


def pack_kernel(plan, y_blocks, out, sem, *, rows):
    me = plan[1, 0, ME]
    started = jnp.int32(0)
    for r in range(rows):
        count = jnp.where(me == r, 0, plan[1, r, 0])

        @pl.loop(0, count)
        def _(j):
            pltpu.make_async_copy(y_blocks.at[plan[0, r, j]], out.at[r, j], sem).start()

        started = started + count

    @pl.loop(0, started)
    def _(_):
        pltpu.make_async_copy(y_blocks.at[0], out.at[0, 0], sem).wait()


def nothing_kernel(*out):
    pass


def product_kernel(plan, x_near, x_far, y_blocks, *refs, targets):
    got, (out, x_held, y_held, sums, into, in_sem, out_sem) = refs[:-7], refs[-7:]
    me, pick, total = plan[2, TOTAL, ME], plan[2, TOTAL, PICK], plan[2, TOTAL, 0]

    for i, brought in enumerate(got):

        @pl.when(pick == i)
        def _():
            @pl.loop(0, total)
            def _(n):
                place, owner = plan[2, X_PLACE, n], plan[2, OWNER, n]
                near, here = plan[2, X_NEAR, n] > 0, owner == me
                sem = in_sem.at[n // TOGETHER]

                @pl.when(near)
                def _():
                    pltpu.make_async_copy(x_near.at[place], x_held.at[n], sem).start()

                @pl.when(jnp.logical_not(near))
                def _():
                    pltpu.make_async_copy(x_far.at[place], x_held.at[n], sem).start()

                @pl.when(here)
                def _():
                    pltpu.make_async_copy(
                        y_blocks.at[plan[2, INNER, n]], y_held.at[n], sem
                    ).start()

                @pl.when(jnp.logical_not(here))
                def _():
                    pltpu.make_async_copy(
                        brought.at[owner, plan[2, SLOT, n]], y_held.at[n], sem
                    ).start()

                into[n] = plan[2, TARGET, n]

    for j in range(TOGETHER - 1):
        into[total + j] = targets
    sums[...] = jnp.zeros_like(sums)
    dot = functools.partial(jnp.dot, preferred_element_type=jnp.float32)

    @pl.loop(0, (total + TOGETHER - 1) // TOGETHER)
    def _(i):
        n = i * TOGETHER
        for j in range(TOGETHER):

            @pl.when(n + j < total)
            def _():
                pltpu.make_async_copy(x_near.at[0], x_held.at[n + j], in_sem.at[i]).wait()
                pltpu.make_async_copy(y_blocks.at[0], y_held.at[n + j], in_sem.at[i]).wait()

        products = []
        for j in range(TOGETHER):
            x, y = x_held[n + j], y_held[n + j]
            x_hi, y_hi = x.astype(jnp.bfloat16), y.astype(jnp.bfloat16)
            x_lo = (x - x_hi.astype(jnp.float32)).astype(jnp.bfloat16)
            y_lo = (y - y_hi.astype(jnp.float32)).astype(jnp.bfloat16)
            products.append(
                dot(
                    jnp.concatenate([x_hi, x_lo, x_hi], axis=1),
                    jnp.concatenate([y_hi, y_hi, y_lo], axis=0),
                )
            )
        for j in range(TOGETHER):
            sums[into[n + j]] += products[j]

    for s in range(targets):
        pltpu.make_async_copy(sums.at[plan[2, FIRST, s]], out.at[s], out_sem).start()
    for s in range(targets):
        pltpu.make_async_copy(sums.at[0], out.at[s], out_sem).wait()


def local(x_blocks, x_rows, x_cols, y_blocks, y_cols, z_rows, z_cols):
    row_axes, col_axes = ("x", "y_hi"), ("y_lo", "z", "core")
    rows, cols = lax.axis_size(row_axes), lax.axis_size(col_axes)
    x_blocks = x_blocks[0]
    y_blocks = y_blocks[:, 0]
    per_cell, edge = x_blocks.shape[0], x_blocks.shape[-1]
    panel_rows = y_blocks.shape[0]
    targets = z_rows.shape[1]
    group = cols * per_cell // rows
    cell_width = panel_rows * rows // cols
    half = cols // 2
    block = (edge, edge)

    own = jnp.pad(jnp.concatenate([x_rows[0], x_cols[0]]), (0, LANES - 2 * per_cell))
    own = jnp.broadcast_to(own, (cols, 1, LANES))
    rest = jnp.stack(
        [jnp.pad(v, (0, LANES - v.shape[0])) for v in (z_rows[0], z_cols[0], y_cols[:, 0])]
    )
    own, x_blocks = lax.optimization_barrier((own, x_blocks))
    panel = lax.all_to_all(own, col_axes, 0, 0, tiled=True).reshape(cols, LANES)
    panel, rest = lax.optimization_barrier((panel, rest))

    across = lax.ppermute(x_blocks, "y_lo", [(0, 1), (1, 0)])
    x_near = lax.all_gather(x_blocks, ("z", "core"), axis=0, tiled=True)

    sheet = pl.pallas_call(
        functools.partial(sheet_kernel, per_cell=per_cell),
        out_shape=jax.ShapeDtypeStruct((rows, 5, LANES), jnp.int32),
        in_specs=[VMEM] * 2,
        out_specs=VMEM,
        compiler_params=pltpu.CompilerParams(vmem_limit_bytes=4 * 2**20),
        name="sheet",
    )(panel, rest)
    info = lax.all_to_all(sheet, row_axes, 0, 0, tiled=True)
    info, across = lax.optimization_barrier((info, across))
    x_far = lax.all_gather(across, ("z", "core"), axis=0, tiled=True)

    plan, pick = pl.pallas_call(
        functools.partial(
            plan_kernel,
            rows=rows,
            cell_width=cell_width,
            per_cell=per_cell,
            group=group,
            half=half,
            targets=targets,
            panel_rows=panel_rows,
        ),
        out_shape=(
            jax.ShapeDtypeStruct((3, rows, LANES), jnp.int32),
            jax.ShapeDtypeStruct((1,), jnp.int32),
        ),
        in_specs=[VMEM],
        out_specs=(VMEM, SMEM),
        scratch_shapes=[pltpu.VMEM((LANES, LANES), jnp.float32)],
        compiler_params=pltpu.CompilerParams(vmem_limit_bytes=4 * 2**20),
        name="plan",
    )(info)

    def room(slots):
        return jax.ShapeDtypeStruct((rows, slots) + block, jnp.float32)

    def with_slots(slots):
        def branch(plan, y_blocks):
            packed = pl.pallas_call(
                functools.partial(pack_kernel, rows=rows),
                out_shape=room(slots),
                in_specs=[SMEM, HBM],
                out_specs=VMEM,
                scratch_shapes=[pltpu.SemaphoreType.DMA],
                compiler_params=pltpu.CompilerParams(vmem_limit_bytes=40 * 2**20),
                name="pack",
            )(plan, y_blocks)
            others = [s for s in SLOTS if s != slots]
            unused = pl.pallas_call(
                nothing_kernel,
                out_shape=[room(s) for s in others],
                out_specs=[HBM] * len(others),
                name="unused",
            )()
            packed, unused = lax.optimization_barrier((packed, unused))
            unused = dict(zip(others, unused, strict=True))
            got = lax.all_to_all(packed, row_axes, 0, 0, tiled=True)
            return [got if s == slots else unused[s] for s in SLOTS]

        return branch

    got = lax.switch(pick[0], [with_slots(s) for s in SLOTS], plan, y_blocks)

    out = pl.pallas_call(
        functools.partial(product_kernel, targets=targets),
        out_shape=jax.ShapeDtypeStruct((targets,) + block, jnp.float32),
        in_specs=[SMEM] + [HBM] * (3 + len(SLOTS)),
        out_specs=HBM,
        scratch_shapes=[
            pltpu.VMEM((LANES,) + block, jnp.float32),
            pltpu.VMEM((LANES,) + block, jnp.float32),
            pltpu.VMEM((targets + 1,) + block, jnp.float32),
            pltpu.SMEM((LANES + TOGETHER,), jnp.int32),
            pltpu.SemaphoreType.DMA((LANES // TOGETHER,)),
            pltpu.SemaphoreType.DMA,
        ],
        compiler_params=pltpu.CompilerParams(vmem_limit_bytes=60 * 2**20),
        name="products",
    )(plan, x_near, x_far, y_blocks, *got)
    return out[None]


def solution(mesh):
    chips = Mesh(mesh.devices.reshape(4, 2, 2, 8, 2), ("x", "y_hi", "y_lo", "z", "core"))
    row, col = ("x", "y_hi"), ("y_lo", "z", "core")
    flat, blocks = P(row, col), P(row, col, None, None)
    return jax.shard_map(
        local,
        mesh=chips,
        in_specs=(blocks, flat, flat, blocks, flat, flat, flat),
        out_specs=blocks,
        check_vma=False,
    )
```

```python
import functools

import jax
import jax.numpy as jnp
from jax import lax
from jax.experimental import pallas as pl
from jax.experimental.pallas import tpu as pltpu
from jax.sharding import Mesh
from jax.sharding import PartitionSpec as P

LANES = 128
SLOTS = (5, 6, 7, 8, 9, 10, 11, 12, 14, 16)
TOGETHER = 8
HBM = pl.BlockSpec(memory_space=pltpu.HBM)
ANY = pl.BlockSpec(memory_space=pl.ANY)
SMEM = pl.BlockSpec(memory_space=pltpu.SMEM)
VMEM = pl.BlockSpec(memory_space=pltpu.VMEM)


X_PLACE, OWNER, SLOT, TARGET, INNER, TOTAL, FIRST = range(7)
ME, PICK = 126, 127


def sheet_kernel(panel, rest, sheet, *, per_cell):
    cols = panel.shape[0]
    got = panel[...].astype(jnp.float32)
    lane = lax.broadcasted_iota(jnp.int32, (LANES, LANES), 1)
    up = lax.broadcasted_iota(jnp.int32, (LANES, LANES), 0)
    cell = lax.broadcasted_iota(jnp.int32, (cols, LANES), 0)
    mine = cell == lax.broadcasted_iota(jnp.int32, (cols, LANES), 1) // per_cell
    lines = []
    for base in (0, per_cell):
        repeated = jnp.dot(
            got,
            (up == base + lane % per_cell).astype(jnp.float32),
            preferred_element_type=jnp.float32,
        )
        lines.append(jnp.sum(jnp.where(mine, repeated, 0.0), axis=0, keepdims=True))
    whole = jnp.concatenate([v.astype(jnp.int32) for v in lines] + [rest[...]], axis=0)
    for r in range(sheet.shape[0]):
        sheet[r] = whole


def plan_kernel(
    info, plan, pick, spread, *, rows, cell_width, per_cell, group, half, targets, panel_rows
):
    shape = (rows, LANES)
    lane = lax.broadcasted_iota(jnp.int32, shape, 1)
    row = lax.broadcasted_iota(jnp.int32, shape, 0)
    x_row, x_col = info[:, 0, :], info[:, 1, :]
    z_code = info[:, 2, :] * cell_width + info[:, 3, :]
    y_col = info[:, 4, :].astype(jnp.float32)
    owner = lane // group
    inner = (lane // per_cell) % (group // per_cell) * cell_width + x_col
    spread[...] = lax.dot_general(
        y_col,
        (row == owner).astype(jnp.float32),
        (((0,), (0,)), ((), ())),
        preferred_element_type=jnp.float32,
    )
    met = jnp.zeros(shape, jnp.float32)
    for k in range(panel_rows):
        met = jnp.where(inner == k, spread[k : k + 1, :], met)
    code = x_row * cell_width + met.astype(jnp.int32)
    target = jnp.full(shape, -1, jnp.int32)
    first = lane
    for s in reversed(range(targets)):
        wanted = z_code[:, s : s + 1]
        target = jnp.where(code == wanted, s, target)
        first = jnp.where(z_code == wanted, s, first)
    used = target >= 0
    key = jnp.where(used, inner, -1 - lane)
    place = lane % group
    repeat = jnp.zeros(shape, jnp.int32)
    for d in range(1, group):
        same = (pltpu.roll(key, d, 1) == key) & (place >= d)
        repeat = jnp.where(same, d, repeat)
    sent = used & (repeat == 0)
    sent_f = sent.astype(jnp.float32)
    up = lax.broadcasted_iota(jnp.int32, (LANES, LANES), 0)
    across = lax.broadcasted_iota(jnp.int32, (LANES, LANES), 1)
    together = (up // group) == (across // group)
    before = (together & (up < across)).astype(jnp.float32)
    slot = jnp.dot(sent_f, before, preferred_element_type=jnp.float32).astype(jnp.int32)
    count = jnp.dot(sent_f, together.astype(jnp.float32), preferred_element_type=jnp.float32)
    held = slot
    for d in range(1, group):
        held = jnp.where(repeat == d, pltpu.roll(slot, d, 1), held)
    me = lax.axis_index("x") * lax.axis_size("y_hi") + lax.axis_index("y_hi")
    side = lax.axis_index("y_lo")

    own_first = (LANES - group * me) % LANES
    mine = lambda v: pltpu.roll(v, own_first, 1)
    sent_slot, sent_row = mine(jnp.where(sent, slot, -1)), mine(inner)
    blocks = jnp.zeros(shape, jnp.int32)
    for t in range(group):
        blocks = jnp.where(lane == sent_slot[:, t : t + 1], sent_row[:, t : t + 1], blocks)
    plan[0] = blocks
    plan[1] = jnp.where(lane == ME, me, mine(count.astype(jnp.int32)))

    def own(v):
        return jnp.sum(jnp.where(row == me, v.astype(jnp.float32), 0.0), axis=0, keepdims=True)

    used_f = used.astype(jnp.float32)
    rank = jnp.dot(used_f, (up < across).astype(jnp.float32), preferred_element_type=jnp.float32)
    chosen = (own(rank).astype(jnp.int32) == up) & (own(used_f) > 0.0)
    p = lane[:1]
    cell = p // per_cell
    facts = jnp.concatenate(
        [
            (
                cell % half * (2 * per_cell)
                + jnp.where(cell // half == side, 0, per_cell)
                + p % per_cell
            ).astype(jnp.float32),
            owner[:1].astype(jnp.float32),
            own(held),
            own(target),
            own(inner),
            jnp.zeros((3, LANES), jnp.float32),
        ]
    )
    listed = lax.dot_general(
        facts,
        chosen.astype(jnp.float32),
        (((1,), (1,)), ((), ())),
        preferred_element_type=jnp.float32,
    )
    total = jnp.sum(own(used_f), axis=1, keepdims=True)
    most = jnp.max(jnp.where(owner == row, 0.0, count)).astype(jnp.int32)
    choice = jnp.int32(0)
    for limit in SLOTS[:-1]:
        choice = choice + (most > limit).astype(jnp.int32)
    pick[0] = choice
    scalars = jnp.where(
        lane == ME, me.astype(jnp.float32), jnp.where(lane == PICK, choice.astype(jnp.float32), total)
    )
    plan[2] = jnp.where(
        row == TOTAL, scalars, jnp.where(row == FIRST, own(first), listed)
    ).astype(jnp.int32)


def pack_kernel(plan, y_blocks, out, sem, *, rows):
    me = plan[1, 0, ME]
    started = jnp.int32(0)
    for r in range(rows):
        count = jnp.where(me == r, 0, plan[1, r, 0])

        @pl.loop(0, count)
        def _(j):
            pltpu.make_async_copy(y_blocks.at[plan[0, r, j]], out.at[r, j], sem).start()

        started = started + count

    @pl.loop(0, started)
    def _(_):
        pltpu.make_async_copy(y_blocks.at[0], out.at[0, 0], sem).wait()


def nothing_kernel(*out):
    pass


def product_kernel(plan, x_all, y_blocks, *refs, targets):
    got, (out, x_held, y_held, sums, into, in_sem, out_sem) = refs[:-7], refs[-7:]
    me, pick, total = plan[2, TOTAL, ME], plan[2, TOTAL, PICK], plan[2, TOTAL, 0]

    for i, brought in enumerate(got):

        @pl.when(pick == i)
        def _():
            @pl.loop(0, total)
            def _(n):
                place, owner = plan[2, X_PLACE, n], plan[2, OWNER, n]
                here = owner == me
                sem = in_sem.at[n // TOGETHER]
                pltpu.make_async_copy(x_all.at[place], x_held.at[n], sem).start()

                @pl.when(here)
                def _():
                    pltpu.make_async_copy(
                        y_blocks.at[plan[2, INNER, n]], y_held.at[n], sem
                    ).start()

                @pl.when(jnp.logical_not(here))
                def _():
                    pltpu.make_async_copy(
                        brought.at[owner, plan[2, SLOT, n]], y_held.at[n], sem
                    ).start()

                into[n] = plan[2, TARGET, n]

    for j in range(TOGETHER - 1):
        into[total + j] = targets
    sums[...] = jnp.zeros_like(sums)
    dot = functools.partial(jnp.dot, preferred_element_type=jnp.float32)

    @pl.loop(0, (total + TOGETHER - 1) // TOGETHER)
    def _(i):
        n = i * TOGETHER
        for j in range(TOGETHER):

            @pl.when(n + j < total)
            def _():
                pltpu.make_async_copy(x_all.at[0], x_held.at[n + j], in_sem.at[i]).wait()
                pltpu.make_async_copy(y_blocks.at[0], y_held.at[n + j], in_sem.at[i]).wait()

        products = []
        for j in range(TOGETHER):
            x, y = x_held[n + j], y_held[n + j]
            x_hi, y_hi = x.astype(jnp.bfloat16), y.astype(jnp.bfloat16)
            x_lo = (x - x_hi.astype(jnp.float32)).astype(jnp.bfloat16)
            y_lo = (y - y_hi.astype(jnp.float32)).astype(jnp.bfloat16)
            products.append(
                dot(
                    jnp.concatenate([x_hi, x_lo, x_hi], axis=1),
                    jnp.concatenate([y_hi, y_hi, y_lo], axis=0),
                )
            )
        for j in range(TOGETHER):
            sums[into[n + j]] += products[j]

    for s in range(targets):
        pltpu.make_async_copy(sums.at[plan[2, FIRST, s]], out.at[s], out_sem).start()
    for s in range(targets):
        pltpu.make_async_copy(sums.at[0], out.at[s], out_sem).wait()


def local(x_blocks, x_rows, x_cols, y_blocks, y_cols, z_rows, z_cols):
    row_axes, col_axes = ("x", "y_hi"), ("y_lo", "z", "core")
    rows, cols = lax.axis_size(row_axes), lax.axis_size(col_axes)
    x_blocks = x_blocks[0]
    y_blocks = y_blocks[:, 0]
    per_cell, edge = x_blocks.shape[0], x_blocks.shape[-1]
    panel_rows = y_blocks.shape[0]
    targets = z_rows.shape[1]
    group = cols * per_cell // rows
    cell_width = panel_rows * rows // cols
    half = cols // 2
    block = (edge, edge)

    own = jnp.pad(jnp.concatenate([x_rows[0], x_cols[0]]), (0, LANES - 2 * per_cell))
    own = jnp.broadcast_to(own, (cols, 1, LANES))
    rest = jnp.stack(
        [jnp.pad(v, (0, LANES - v.shape[0])) for v in (z_rows[0], z_cols[0], y_cols[:, 0])]
    )
    own, x_blocks = lax.optimization_barrier((own, x_blocks))
    panel = lax.all_to_all(own, col_axes, 0, 0, tiled=True).reshape(cols, LANES)

    across = lax.ppermute(x_blocks, "y_lo", [(0, 1), (1, 0)])
    pair = jnp.concatenate([x_blocks, across], axis=0)
    panel, rest, pair = lax.optimization_barrier((panel, rest, pair))
    x_all = lax.all_gather(pair, ("z", "core"), axis=0, tiled=True)

    sheet = pl.pallas_call(
        functools.partial(sheet_kernel, per_cell=per_cell),
        out_shape=jax.ShapeDtypeStruct((rows, 5, LANES), jnp.int32),
        in_specs=[VMEM] * 2,
        out_specs=VMEM,
        compiler_params=pltpu.CompilerParams(vmem_limit_bytes=4 * 2**20),
        name="sheet",
    )(panel, rest)
    info = lax.all_to_all(sheet, row_axes, 0, 0, tiled=True)

    plan, pick = pl.pallas_call(
        functools.partial(
            plan_kernel,
            rows=rows,
            cell_width=cell_width,
            per_cell=per_cell,
            group=group,
            half=half,
            targets=targets,
            panel_rows=panel_rows,
        ),
        out_shape=(
            jax.ShapeDtypeStruct((3, rows, LANES), jnp.int32),
            jax.ShapeDtypeStruct((1,), jnp.int32),
        ),
        in_specs=[VMEM],
        out_specs=(VMEM, SMEM),
        scratch_shapes=[pltpu.VMEM((LANES, LANES), jnp.float32)],
        compiler_params=pltpu.CompilerParams(vmem_limit_bytes=4 * 2**20),
        name="plan",
    )(info)

    def room(slots):
        return jax.ShapeDtypeStruct((rows, slots) + block, jnp.float32)

    def with_slots(slots):
        def branch(plan, y_blocks):
            packed = pl.pallas_call(
                functools.partial(pack_kernel, rows=rows),
                out_shape=room(slots),
                in_specs=[SMEM, HBM],
                out_specs=VMEM,
                scratch_shapes=[pltpu.SemaphoreType.DMA],
                compiler_params=pltpu.CompilerParams(vmem_limit_bytes=40 * 2**20),
                name="pack",
            )(plan, y_blocks)
            others = [s for s in SLOTS if s != slots]
            unused = pl.pallas_call(
                nothing_kernel,
                out_shape=[room(s) for s in others],
                out_specs=[HBM] * len(others),
                name="unused",
            )()
            packed, unused = lax.optimization_barrier((packed, unused))
            unused = dict(zip(others, unused, strict=True))
            got = lax.all_to_all(packed, row_axes, 0, 0, tiled=True)
            return [got if s == slots else unused[s] for s in SLOTS]

        return branch

    got = lax.switch(pick[0], [with_slots(s) for s in SLOTS], plan, y_blocks)

    out = pl.pallas_call(
        functools.partial(product_kernel, targets=targets),
        out_shape=jax.ShapeDtypeStruct((targets,) + block, jnp.float32),
        in_specs=[SMEM] + [HBM] * (2 + len(SLOTS)),
        out_specs=HBM,
        scratch_shapes=[
            pltpu.VMEM((LANES,) + block, jnp.float32),
            pltpu.VMEM((LANES,) + block, jnp.float32),
            pltpu.VMEM((targets + 1,) + block, jnp.float32),
            pltpu.SMEM((LANES + TOGETHER,), jnp.int32),
            pltpu.SemaphoreType.DMA((LANES // TOGETHER,)),
            pltpu.SemaphoreType.DMA,
        ],
        compiler_params=pltpu.CompilerParams(vmem_limit_bytes=60 * 2**20),
        name="products",
    )(plan, x_all, y_blocks, *got)
    return out[None]


def solution(mesh):
    chips = Mesh(mesh.devices.reshape(4, 2, 2, 8, 2), ("x", "y_hi", "y_lo", "z", "core"))
    row, col = ("x", "y_hi"), ("y_lo", "z", "core")
    flat, blocks = P(row, col), P(row, col, None, None)
    return jax.shard_map(
        local,
        mesh=chips,
        in_specs=(blocks, flat, flat, blocks, flat, flat, flat),
        out_specs=blocks,
        check_vma=False,
    )
```

```python
import functools

import jax
import jax.numpy as jnp
from jax import lax
from jax.experimental import pallas as pl
from jax.experimental.pallas import tpu as pltpu
from jax.sharding import Mesh
from jax.sharding import PartitionSpec as P

LANES = 128
SLOTS = (5, 6, 7, 8, 9, 10, 11, 12, 14, 16)
TOGETHER = 8
HBM = pl.BlockSpec(memory_space=pltpu.HBM)
ANY = pl.BlockSpec(memory_space=pl.ANY)
SMEM = pl.BlockSpec(memory_space=pltpu.SMEM)
VMEM = pl.BlockSpec(memory_space=pltpu.VMEM)


X_PLACE, OWNER, SLOT, TARGET, INNER, TOTAL, FIRST = range(7)
ME, PICK, BASE = 126, 127, 125
BASES, EXTRA = (8, 9, 10), 2


def sheet_kernel(panel, rest, sheet, *, per_cell):
    cols = panel.shape[0]
    got = panel[...].astype(jnp.float32)
    lane = lax.broadcasted_iota(jnp.int32, (LANES, LANES), 1)
    up = lax.broadcasted_iota(jnp.int32, (LANES, LANES), 0)
    cell = lax.broadcasted_iota(jnp.int32, (cols, LANES), 0)
    mine = cell == lax.broadcasted_iota(jnp.int32, (cols, LANES), 1) // per_cell
    lines = []
    for base in (0, per_cell):
        repeated = jnp.dot(
            got,
            (up == base + lane % per_cell).astype(jnp.float32),
            preferred_element_type=jnp.float32,
        )
        lines.append(jnp.sum(jnp.where(mine, repeated, 0.0), axis=0, keepdims=True))
    whole = jnp.concatenate([v.astype(jnp.int32) for v in lines] + [rest[...]], axis=0)
    for r in range(sheet.shape[0]):
        sheet[r] = whole


def plan_kernel(
    info, plan, pick, spread, *, rows, cell_width, per_cell, group, half, targets, panel_rows
):
    shape = (rows, LANES)
    lane = lax.broadcasted_iota(jnp.int32, shape, 1)
    row = lax.broadcasted_iota(jnp.int32, shape, 0)
    x_row, x_col = info[:, 0, :], info[:, 1, :]
    z_code = info[:, 2, :] * cell_width + info[:, 3, :]
    y_col = info[:, 4, :].astype(jnp.float32)
    owner = lane // group
    inner = (lane // per_cell) % (group // per_cell) * cell_width + x_col
    spread[...] = lax.dot_general(
        y_col,
        (row == owner).astype(jnp.float32),
        (((0,), (0,)), ((), ())),
        preferred_element_type=jnp.float32,
    )
    met = jnp.zeros(shape, jnp.float32)
    for k in range(panel_rows):
        met = jnp.where(inner == k, spread[k : k + 1, :], met)
    code = x_row * cell_width + met.astype(jnp.int32)
    target = jnp.full(shape, -1, jnp.int32)
    first = lane
    for s in reversed(range(targets)):
        wanted = z_code[:, s : s + 1]
        target = jnp.where(code == wanted, s, target)
        first = jnp.where(z_code == wanted, s, first)
    used = target >= 0
    key = jnp.where(used, inner, -1 - lane)
    place = lane % group
    repeat = jnp.zeros(shape, jnp.int32)
    for d in range(1, group):
        same = (pltpu.roll(key, d, 1) == key) & (place >= d)
        repeat = jnp.where(same, d, repeat)
    sent = used & (repeat == 0)
    sent_f = sent.astype(jnp.float32)
    up = lax.broadcasted_iota(jnp.int32, (LANES, LANES), 0)
    across = lax.broadcasted_iota(jnp.int32, (LANES, LANES), 1)
    together = (up // group) == (across // group)
    before = (together & (up < across)).astype(jnp.float32)
    slot = jnp.dot(sent_f, before, preferred_element_type=jnp.float32).astype(jnp.int32)
    count = jnp.dot(sent_f, together.astype(jnp.float32), preferred_element_type=jnp.float32)
    held = slot
    for d in range(1, group):
        held = jnp.where(repeat == d, pltpu.roll(slot, d, 1), held)
    me = lax.axis_index("x") * lax.axis_size("y_hi") + lax.axis_index("y_hi")
    side = lax.axis_index("y_lo")

    own_first = (LANES - group * me) % LANES
    mine = lambda v: pltpu.roll(v, own_first, 1)
    sent_slot, sent_row = mine(jnp.where(sent, slot, -1)), mine(inner)
    blocks = jnp.zeros(shape, jnp.int32)
    for t in range(group):
        blocks = jnp.where(lane == sent_slot[:, t : t + 1], sent_row[:, t : t + 1], blocks)
    plan[0] = blocks
    plan[1] = jnp.where(lane == ME, me, mine(count.astype(jnp.int32)))

    def own(v):
        return jnp.sum(jnp.where(row == me, v.astype(jnp.float32), 0.0), axis=0, keepdims=True)

    used_f = used.astype(jnp.float32)
    rank = jnp.dot(used_f, (up < across).astype(jnp.float32), preferred_element_type=jnp.float32)
    chosen = (own(rank).astype(jnp.int32) == up) & (own(used_f) > 0.0)
    p = lane[:1]
    cell = p // per_cell
    facts = jnp.concatenate(
        [
            (
                cell % half * (2 * per_cell)
                + jnp.where(cell // half == side, 0, per_cell)
                + p % per_cell
            ).astype(jnp.float32),
            owner[:1].astype(jnp.float32),
            own(held),
            own(target),
            own(inner),
            jnp.zeros((3, LANES), jnp.float32),
        ]
    )
    listed = lax.dot_general(
        facts,
        chosen.astype(jnp.float32),
        (((1,), (1,)), ((), ())),
        preferred_element_type=jnp.float32,
    )
    total = jnp.sum(own(used_f), axis=1, keepdims=True)
    needed = jnp.where(owner == row, 0, count.astype(jnp.int32))
    most = jnp.max(needed)
    slots = jnp.int32(0)
    for limit in SLOTS[:-1]:
        slots = slots + (most > limit).astype(jnp.int32)
    base, choice = jnp.int32(SLOTS[-1]), slots
    apart = (row - owner + rows) % rows
    for i, few in reversed(list(enumerate(BASES))):
        over = needed > few
        nearest = jnp.min(jnp.where(over, apart, rows))
        only = jnp.max(jnp.where(over, apart, 0)) == nearest
        fits = only & (most <= few + EXTRA)
        slots = jnp.where(fits, SLOTS.index(few), slots)
        base = jnp.where(fits, few, base)
        choice = jnp.where(fits, len(SLOTS) + (rows - 1) * i + nearest - 1, choice)
    pick[0] = choice
    scalars = total.astype(jnp.int32)
    for at, v in ((ME, me), (PICK, slots), (BASE, base)):
        scalars = jnp.where(lane == at, v, scalars)
    scalars = scalars.astype(jnp.float32)
    plan[2] = jnp.where(
        row == TOTAL, scalars, jnp.where(row == FIRST, own(first), listed)
    ).astype(jnp.int32)


def pack_kernel(plan, y_blocks, out, sem, *, rows):
    me, slots = plan[1, 0, ME], out.shape[1]
    started = jnp.int32(0)
    for r in range(rows):
        count = jnp.where(me == r, 0, jnp.minimum(plan[1, r, 0], slots))

        @pl.loop(0, count)
        def _(j):
            pltpu.make_async_copy(y_blocks.at[plan[0, r, j]], out.at[r, j], sem).start()

        started = started + count

    @pl.loop(0, started)
    def _(_):
        pltpu.make_async_copy(y_blocks.at[0], out.at[0, 0], sem).wait()


def pack_extra_kernel(plan, y_blocks, out, sem, *, rows, slots, apart):
    r = (plan[1, 0, ME] + apart) % rows
    count = jnp.clip(plan[1, r, 0] - slots, 0, EXTRA)

    @pl.loop(0, count)
    def _(j):
        pltpu.make_async_copy(y_blocks.at[plan[0, r, slots + j]], out.at[j], sem).start()

    @pl.loop(0, count)
    def _(j):
        pltpu.make_async_copy(y_blocks.at[0], out.at[j], sem).wait()


def nothing_kernel(*out):
    pass


def product_kernel(plan, x_all, y_blocks, extra, *refs, targets):
    got, (out, x_held, y_held, sums, into, in_sem, out_sem) = refs[:-7], refs[-7:]
    base = plan[2, TOTAL, BASE]
    me, pick, total = plan[2, TOTAL, ME], plan[2, TOTAL, PICK], plan[2, TOTAL, 0]

    for i, brought in enumerate(got):

        @pl.when(pick == i)
        def _():
            @pl.loop(0, total)
            def _(n):
                place, owner = plan[2, X_PLACE, n], plan[2, OWNER, n]
                here = owner == me
                sem = in_sem.at[n // TOGETHER]
                pltpu.make_async_copy(x_all.at[place], x_held.at[n], sem).start()

                @pl.when(here)
                def _():
                    pltpu.make_async_copy(
                        y_blocks.at[plan[2, INNER, n]], y_held.at[n], sem
                    ).start()

                slot = plan[2, SLOT, n]

                @pl.when(jnp.logical_not(here) & (slot < base))
                def _():
                    pltpu.make_async_copy(brought.at[owner, slot], y_held.at[n], sem).start()

                @pl.when(jnp.logical_not(here) & (slot >= base))
                def _():
                    pltpu.make_async_copy(extra.at[slot - base], y_held.at[n], sem).start()

                into[n] = plan[2, TARGET, n]

    for j in range(TOGETHER - 1):
        into[total + j] = targets
    sums[...] = jnp.zeros_like(sums)
    dot = functools.partial(jnp.dot, preferred_element_type=jnp.float32)

    @pl.loop(0, (total + TOGETHER - 1) // TOGETHER)
    def _(i):
        n = i * TOGETHER
        for j in range(TOGETHER):

            @pl.when(n + j < total)
            def _():
                pltpu.make_async_copy(x_all.at[0], x_held.at[n + j], in_sem.at[i]).wait()
                pltpu.make_async_copy(y_blocks.at[0], y_held.at[n + j], in_sem.at[i]).wait()

        products = []
        for j in range(TOGETHER):
            x, y = x_held[n + j], y_held[n + j]
            x_hi, y_hi = x.astype(jnp.bfloat16), y.astype(jnp.bfloat16)
            x_lo = (x - x_hi.astype(jnp.float32)).astype(jnp.bfloat16)
            y_lo = (y - y_hi.astype(jnp.float32)).astype(jnp.bfloat16)
            products.append(
                dot(
                    jnp.concatenate([x_hi, x_lo, x_hi], axis=1),
                    jnp.concatenate([y_hi, y_hi, y_lo], axis=0),
                )
            )
        for j in range(TOGETHER):
            sums[into[n + j]] += products[j]

    for s in range(targets):
        pltpu.make_async_copy(sums.at[plan[2, FIRST, s]], out.at[s], out_sem).start()
    for s in range(targets):
        pltpu.make_async_copy(sums.at[0], out.at[s], out_sem).wait()


def local(x_blocks, x_rows, x_cols, y_blocks, y_cols, z_rows, z_cols):
    row_axes, col_axes = ("x", "y_hi"), ("y_lo", "z", "core")
    rows, cols = lax.axis_size(row_axes), lax.axis_size(col_axes)
    x_blocks = x_blocks[0]
    y_blocks = y_blocks[:, 0]
    per_cell, edge = x_blocks.shape[0], x_blocks.shape[-1]
    panel_rows = y_blocks.shape[0]
    targets = z_rows.shape[1]
    group = cols * per_cell // rows
    cell_width = panel_rows * rows // cols
    half = cols // 2
    block = (edge, edge)

    own = jnp.pad(jnp.concatenate([x_rows[0], x_cols[0]]), (0, LANES - 2 * per_cell))
    own = jnp.broadcast_to(own, (cols, 1, LANES))
    rest = jnp.stack(
        [jnp.pad(v, (0, LANES - v.shape[0])) for v in (z_rows[0], z_cols[0], y_cols[:, 0])]
    )
    own, x_blocks = lax.optimization_barrier((own, x_blocks))
    panel = lax.all_to_all(own, col_axes, 0, 0, tiled=True).reshape(cols, LANES)

    across = lax.ppermute(x_blocks, "y_lo", [(0, 1), (1, 0)])
    pair = jnp.concatenate([x_blocks, across], axis=0)
    panel, rest, pair = lax.optimization_barrier((panel, rest, pair))
    x_all = lax.all_gather(pair, ("z", "core"), axis=0, tiled=True)

    sheet = pl.pallas_call(
        functools.partial(sheet_kernel, per_cell=per_cell),
        out_shape=jax.ShapeDtypeStruct((rows, 5, LANES), jnp.int32),
        in_specs=[VMEM] * 2,
        out_specs=VMEM,
        compiler_params=pltpu.CompilerParams(vmem_limit_bytes=4 * 2**20),
        name="sheet",
    )(panel, rest)
    info = lax.all_to_all(sheet, row_axes, 0, 0, tiled=True)

    plan, pick = pl.pallas_call(
        functools.partial(
            plan_kernel,
            rows=rows,
            cell_width=cell_width,
            per_cell=per_cell,
            group=group,
            half=half,
            targets=targets,
            panel_rows=panel_rows,
        ),
        out_shape=(
            jax.ShapeDtypeStruct((3, rows, LANES), jnp.int32),
            jax.ShapeDtypeStruct((1,), jnp.int32),
        ),
        in_specs=[VMEM],
        out_specs=(VMEM, SMEM),
        scratch_shapes=[pltpu.VMEM((LANES, LANES), jnp.float32)],
        compiler_params=pltpu.CompilerParams(vmem_limit_bytes=4 * 2**20),
        name="plan",
    )(info)

    def room(slots):
        return jax.ShapeDtypeStruct((rows, slots) + block, jnp.float32)

    more = jax.ShapeDtypeStruct((EXTRA,) + block, jnp.float32)

    def pack(kernel, shape, plan, y_blocks):
        return pl.pallas_call(
            functools.partial(kernel, rows=rows),
            out_shape=shape,
            in_specs=[SMEM, HBM],
            out_specs=VMEM,
            scratch_shapes=[pltpu.SemaphoreType.DMA],
            compiler_params=pltpu.CompilerParams(vmem_limit_bytes=40 * 2**20),
            name="pack",
        )(plan, y_blocks)

    def nothing(shapes):
        return pl.pallas_call(
            nothing_kernel, out_shape=shapes, out_specs=[HBM] * len(shapes), name="unused"
        )()

    def with_slots(slots, apart=0):
        def exchange(plan, y_blocks):
            packed = pack(pack_kernel, room(slots), plan, y_blocks)
            return lax.all_to_all(packed, row_axes, 0, 0, tiled=True)

        def branch(plan, chosen, y_blocks):
            others = [s for s in SLOTS if s != slots]
            unused = nothing([room(s) for s in others] + [more] * (apart == 0))
            plan, unused = lax.optimization_barrier((plan, unused))
            got = dict(zip(others, unused))
            if apart:
                kernel = functools.partial(pack_extra_kernel, slots=slots, apart=apart)
                extra = pack(kernel, more, plan, y_blocks)
                plan, extra = lax.optimization_barrier((plan, extra))
                turn = [(i, (i + apart) % rows) for i in range(rows)]
                extra = lax.ppermute(extra, row_axes, turn)
                got[slots] = lax.cond(
                    chosen >= 0, exchange, lambda *_: nothing([room(slots)])[0], plan, y_blocks
                )
            else:
                extra = unused[-1]
                got[slots] = exchange(plan, y_blocks)
            return [extra] + [got[s] for s in SLOTS]

        return branch

    branches = [with_slots(s) for s in SLOTS]
    branches += [with_slots(s, apart) for s in BASES for apart in range(1, rows)]

    got = lax.switch(pick[0], branches, plan, pick[0], y_blocks)

    out = pl.pallas_call(
        functools.partial(product_kernel, targets=targets),
        out_shape=jax.ShapeDtypeStruct((targets,) + block, jnp.float32),
        in_specs=[SMEM] + [HBM] * (3 + len(SLOTS)),
        out_specs=HBM,
        scratch_shapes=[
            pltpu.VMEM((LANES,) + block, jnp.float32),
            pltpu.VMEM((LANES,) + block, jnp.float32),
            pltpu.VMEM((targets + 1,) + block, jnp.float32),
            pltpu.SMEM((LANES + TOGETHER,), jnp.int32),
            pltpu.SemaphoreType.DMA((LANES // TOGETHER,)),
            pltpu.SemaphoreType.DMA,
        ],
        compiler_params=pltpu.CompilerParams(vmem_limit_bytes=60 * 2**20),
        name="products",
    )(plan, x_all, y_blocks, *got)
    return out[None]


def solution(mesh):
    chips = Mesh(mesh.devices.reshape(4, 2, 2, 8, 2), ("x", "y_hi", "y_lo", "z", "core"))
    row, col = ("x", "y_hi"), ("y_lo", "z", "core")
    flat, blocks = P(row, col), P(row, col, None, None)
    return jax.shard_map(
        local,
        mesh=chips,
        in_specs=(blocks, flat, flat, blocks, flat, flat, flat),
        out_specs=blocks,
        check_vma=False,
    )
```

```python
import functools

import jax
import jax.numpy as jnp
from jax import lax
from jax.experimental import pallas as pl
from jax.experimental.pallas import tpu as pltpu
from jax.sharding import Mesh
from jax.sharding import PartitionSpec as P

LANES = 128
SLOTS = (7, 8, 9, 10, 12, 16)
TOGETHER = 8
HBM = pl.BlockSpec(memory_space=pltpu.HBM)
ANY = pl.BlockSpec(memory_space=pl.ANY)
SMEM = pl.BlockSpec(memory_space=pltpu.SMEM)
VMEM = pl.BlockSpec(memory_space=pltpu.VMEM)


X_PLACE, OWNER, SLOT, TARGET, INNER, TOTAL, FIRST = range(7)
ME, PICK, BASE = 126, 127, 125
BASES, EXTRA = (8,), 3


def sheet_kernel(panel, rest, sheet, *, per_cell):
    cols = panel.shape[0]
    got = panel[...].astype(jnp.float32)
    lane = lax.broadcasted_iota(jnp.int32, (LANES, LANES), 1)
    up = lax.broadcasted_iota(jnp.int32, (LANES, LANES), 0)
    cell = lax.broadcasted_iota(jnp.int32, (cols, LANES), 0)
    mine = cell == lax.broadcasted_iota(jnp.int32, (cols, LANES), 1) // per_cell
    lines = []
    for base in (0, per_cell):
        repeated = jnp.dot(
            got,
            (up == base + lane % per_cell).astype(jnp.float32),
            preferred_element_type=jnp.float32,
        )
        lines.append(jnp.sum(jnp.where(mine, repeated, 0.0), axis=0, keepdims=True))
    whole = jnp.concatenate([v.astype(jnp.int32) for v in lines] + [rest[...]], axis=0)
    for r in range(sheet.shape[0]):
        sheet[r] = whole


def plan_kernel(
    info, plan, pick, spread, *, rows, cell_width, per_cell, group, half, targets, panel_rows
):
    shape = (rows, LANES)
    lane = lax.broadcasted_iota(jnp.int32, shape, 1)
    row = lax.broadcasted_iota(jnp.int32, shape, 0)
    x_row, x_col = info[:, 0, :], info[:, 1, :]
    z_code = info[:, 2, :] * cell_width + info[:, 3, :]
    y_col = info[:, 4, :].astype(jnp.float32)
    owner = lane // group
    inner = (lane // per_cell) % (group // per_cell) * cell_width + x_col
    spread[...] = lax.dot_general(
        y_col,
        (row == owner).astype(jnp.float32),
        (((0,), (0,)), ((), ())),
        preferred_element_type=jnp.float32,
    )
    met = jnp.zeros(shape, jnp.float32)
    for k in range(panel_rows):
        met = jnp.where(inner == k, spread[k : k + 1, :], met)
    code = x_row * cell_width + met.astype(jnp.int32)
    target = jnp.full(shape, -1, jnp.int32)
    first = lane
    for s in reversed(range(targets)):
        wanted = z_code[:, s : s + 1]
        target = jnp.where(code == wanted, s, target)
        first = jnp.where(z_code == wanted, s, first)
    used = target >= 0
    key = jnp.where(used, inner, -1 - lane)
    place = lane % group
    repeat = jnp.zeros(shape, jnp.int32)
    for d in range(1, group):
        same = (pltpu.roll(key, d, 1) == key) & (place >= d)
        repeat = jnp.where(same, d, repeat)
    sent = used & (repeat == 0)
    sent_f = sent.astype(jnp.float32)
    up = lax.broadcasted_iota(jnp.int32, (LANES, LANES), 0)
    across = lax.broadcasted_iota(jnp.int32, (LANES, LANES), 1)
    together = (up // group) == (across // group)
    before = (together & (up < across)).astype(jnp.float32)
    slot = jnp.dot(sent_f, before, preferred_element_type=jnp.float32).astype(jnp.int32)
    count = jnp.dot(sent_f, together.astype(jnp.float32), preferred_element_type=jnp.float32)
    held = slot
    for d in range(1, group):
        held = jnp.where(repeat == d, pltpu.roll(slot, d, 1), held)
    me = lax.axis_index("x") * lax.axis_size("y_hi") + lax.axis_index("y_hi")
    side = lax.axis_index("y_lo")

    own_first = (LANES - group * me) % LANES
    mine = lambda v: pltpu.roll(v, own_first, 1)
    sent_slot, sent_row = mine(jnp.where(sent, slot, -1)), mine(inner)
    blocks = jnp.zeros(shape, jnp.int32)
    for t in range(group):
        blocks = jnp.where(lane == sent_slot[:, t : t + 1], sent_row[:, t : t + 1], blocks)
    plan[0] = blocks
    plan[1] = jnp.where(lane == ME, me, mine(count.astype(jnp.int32)))

    def own(v):
        return jnp.sum(jnp.where(row == me, v.astype(jnp.float32), 0.0), axis=0, keepdims=True)

    used_f = used.astype(jnp.float32)
    rank = jnp.dot(used_f, (up < across).astype(jnp.float32), preferred_element_type=jnp.float32)
    chosen = (own(rank).astype(jnp.int32) == up) & (own(used_f) > 0.0)
    p = lane[:1]
    cell = p // per_cell
    facts = jnp.concatenate(
        [
            (
                cell % half * (2 * per_cell)
                + jnp.where(cell // half == side, 0, per_cell)
                + p % per_cell
            ).astype(jnp.float32),
            owner[:1].astype(jnp.float32),
            own(held),
            own(target),
            own(inner),
            jnp.zeros((3, LANES), jnp.float32),
        ]
    )
    listed = lax.dot_general(
        facts,
        chosen.astype(jnp.float32),
        (((1,), (1,)), ((), ())),
        preferred_element_type=jnp.float32,
    )
    total = jnp.sum(own(used_f), axis=1, keepdims=True)
    needed = jnp.where(owner == row, 0, count.astype(jnp.int32))
    most = jnp.max(needed)
    slots = jnp.int32(0)
    for limit in SLOTS[:-1]:
        slots = slots + (most > limit).astype(jnp.int32)
    base, choice = jnp.int32(SLOTS[-1]), slots
    apart = (row - owner + rows) % rows
    for i, few in reversed(list(enumerate(BASES))):
        over = needed > few
        nearest = jnp.min(jnp.where(over, apart, rows))
        only = jnp.max(jnp.where(over, apart, 0)) == nearest
        fits = only & (most <= few + EXTRA)
        slots = jnp.where(fits, SLOTS.index(few), slots)
        base = jnp.where(fits, few, base)
        choice = jnp.where(fits, len(SLOTS) + (rows - 1) * i + nearest - 1, choice)
    pick[0] = choice
    scalars = total.astype(jnp.int32)
    for at, v in ((ME, me), (PICK, slots), (BASE, base)):
        scalars = jnp.where(lane == at, v, scalars)
    scalars = scalars.astype(jnp.float32)
    plan[2] = jnp.where(
        row == TOTAL, scalars, jnp.where(row == FIRST, own(first), listed)
    ).astype(jnp.int32)


def pack_kernel(plan, y_blocks, out, sem, *, rows):
    me, slots = plan[1, 0, ME], out.shape[1]
    started = jnp.int32(0)
    for r in range(rows):
        count = jnp.where(me == r, 0, jnp.minimum(plan[1, r, 0], slots))

        @pl.loop(0, count)
        def _(j):
            pltpu.make_async_copy(y_blocks.at[plan[0, r, j]], out.at[r, j], sem).start()

        started = started + count

    @pl.loop(0, started)
    def _(_):
        pltpu.make_async_copy(y_blocks.at[0], out.at[0, 0], sem).wait()


def pack_extra_kernel(plan, y_blocks, out, sem, *, rows, slots, apart):
    r = (plan[1, 0, ME] + apart) % rows
    count = jnp.clip(plan[1, r, 0] - slots, 0, EXTRA)

    @pl.loop(0, count)
    def _(j):
        pltpu.make_async_copy(y_blocks.at[plan[0, r, slots + j]], out.at[j], sem).start()

    @pl.loop(0, count)
    def _(j):
        pltpu.make_async_copy(y_blocks.at[0], out.at[j], sem).wait()


def nothing_kernel(*out):
    pass


def product_kernel(plan, x_all, y_blocks, extra, *refs, targets):
    got, (out, x_held, y_held, sums, into, in_sem, out_sem) = refs[:-7], refs[-7:]
    base = plan[2, TOTAL, BASE]
    me, pick, total = plan[2, TOTAL, ME], plan[2, TOTAL, PICK], plan[2, TOTAL, 0]

    for i, brought in enumerate(got):

        @pl.when(pick == i)
        def _():
            @pl.loop(0, total)
            def _(n):
                place, owner = plan[2, X_PLACE, n], plan[2, OWNER, n]
                here = owner == me
                sem = in_sem.at[n // TOGETHER]
                pltpu.make_async_copy(x_all.at[place], x_held.at[n], sem).start()

                @pl.when(here)
                def _():
                    pltpu.make_async_copy(
                        y_blocks.at[plan[2, INNER, n]], y_held.at[n], sem
                    ).start()

                slot = plan[2, SLOT, n]

                @pl.when(jnp.logical_not(here) & (slot < base))
                def _():
                    pltpu.make_async_copy(brought.at[owner, slot], y_held.at[n], sem).start()

                @pl.when(jnp.logical_not(here) & (slot >= base))
                def _():
                    pltpu.make_async_copy(extra.at[slot - base], y_held.at[n], sem).start()

                into[n] = plan[2, TARGET, n]

    for j in range(TOGETHER - 1):
        into[total + j] = targets
    sums[...] = jnp.zeros_like(sums)
    dot = functools.partial(jnp.dot, preferred_element_type=jnp.float32)

    @pl.loop(0, (total + TOGETHER - 1) // TOGETHER)
    def _(i):
        n = i * TOGETHER
        for j in range(TOGETHER):

            @pl.when(n + j < total)
            def _():
                pltpu.make_async_copy(x_all.at[0], x_held.at[n + j], in_sem.at[i]).wait()
                pltpu.make_async_copy(y_blocks.at[0], y_held.at[n + j], in_sem.at[i]).wait()

        products = []
        for j in range(TOGETHER):
            x, y = x_held[n + j], y_held[n + j]
            x_hi, y_hi = x.astype(jnp.bfloat16), y.astype(jnp.bfloat16)
            x_lo = (x - x_hi.astype(jnp.float32)).astype(jnp.bfloat16)
            y_lo = (y - y_hi.astype(jnp.float32)).astype(jnp.bfloat16)
            products.append(
                dot(
                    jnp.concatenate([x_hi, x_lo, x_hi], axis=1),
                    jnp.concatenate([y_hi, y_hi, y_lo], axis=0),
                )
            )
        for j in range(TOGETHER):
            sums[into[n + j]] += products[j]

    for s in range(targets):
        pltpu.make_async_copy(sums.at[plan[2, FIRST, s]], out.at[s], out_sem).start()
    for s in range(targets):
        pltpu.make_async_copy(sums.at[0], out.at[s], out_sem).wait()


def local(x_blocks, x_rows, x_cols, y_blocks, y_cols, z_rows, z_cols):
    row_axes, col_axes = ("x", "y_hi"), ("y_lo", "z", "core")
    rows, cols = lax.axis_size(row_axes), lax.axis_size(col_axes)
    x_blocks = x_blocks[0]
    y_blocks = y_blocks[:, 0]
    per_cell, edge = x_blocks.shape[0], x_blocks.shape[-1]
    panel_rows = y_blocks.shape[0]
    targets = z_rows.shape[1]
    group = cols * per_cell // rows
    cell_width = panel_rows * rows // cols
    half = cols // 2
    block = (edge, edge)

    own = jnp.pad(jnp.concatenate([x_rows[0], x_cols[0]]), (0, LANES - 2 * per_cell))
    own = jnp.broadcast_to(own, (cols, 1, LANES))
    rest = jnp.stack(
        [jnp.pad(v, (0, LANES - v.shape[0])) for v in (z_rows[0], z_cols[0], y_cols[:, 0])]
    )
    own, x_blocks = lax.optimization_barrier((own, x_blocks))
    panel = lax.all_to_all(own, col_axes, 0, 0, tiled=True).reshape(cols, LANES)

    across = lax.ppermute(x_blocks, "y_lo", [(0, 1), (1, 0)])
    pair = jnp.concatenate([x_blocks, across], axis=0)
    panel, rest, pair = lax.optimization_barrier((panel, rest, pair))
    x_all = lax.all_gather(pair, ("z", "core"), axis=0, tiled=True)

    sheet = pl.pallas_call(
        functools.partial(sheet_kernel, per_cell=per_cell),
        out_shape=jax.ShapeDtypeStruct((rows, 5, LANES), jnp.int32),
        in_specs=[VMEM] * 2,
        out_specs=VMEM,
        compiler_params=pltpu.CompilerParams(vmem_limit_bytes=4 * 2**20),
        name="sheet",
    )(panel, rest)
    info = lax.all_to_all(sheet, row_axes, 0, 0, tiled=True)

    plan, pick = pl.pallas_call(
        functools.partial(
            plan_kernel,
            rows=rows,
            cell_width=cell_width,
            per_cell=per_cell,
            group=group,
            half=half,
            targets=targets,
            panel_rows=panel_rows,
        ),
        out_shape=(
            jax.ShapeDtypeStruct((3, rows, LANES), jnp.int32),
            jax.ShapeDtypeStruct((1,), jnp.int32),
        ),
        in_specs=[VMEM],
        out_specs=(VMEM, SMEM),
        scratch_shapes=[pltpu.VMEM((LANES, LANES), jnp.float32)],
        compiler_params=pltpu.CompilerParams(vmem_limit_bytes=4 * 2**20),
        name="plan",
    )(info)

    def room(slots):
        return jax.ShapeDtypeStruct((rows, slots) + block, jnp.float32)

    more = jax.ShapeDtypeStruct((EXTRA,) + block, jnp.float32)

    def pack(kernel, shape, plan, y_blocks):
        return pl.pallas_call(
            functools.partial(kernel, rows=rows),
            out_shape=shape,
            in_specs=[SMEM, HBM],
            out_specs=VMEM,
            scratch_shapes=[pltpu.SemaphoreType.DMA],
            compiler_params=pltpu.CompilerParams(vmem_limit_bytes=40 * 2**20),
            name="pack",
        )(plan, y_blocks)

    def nothing(shapes):
        return pl.pallas_call(
            nothing_kernel, out_shape=shapes, out_specs=[HBM] * len(shapes), name="unused"
        )()

    def with_slots(slots, apart=0):
        def exchange(plan, y_blocks):
            packed = pack(pack_kernel, room(slots), plan, y_blocks)
            return lax.all_to_all(packed, row_axes, 0, 0, tiled=True)

        def branch(plan, chosen, y_blocks):
            others = [s for s in SLOTS if s != slots]
            unused = nothing([room(s) for s in others] + [more] * (apart == 0))
            plan, unused = lax.optimization_barrier((plan, unused))
            got = dict(zip(others, unused))
            if apart:
                kernel = functools.partial(pack_extra_kernel, slots=slots, apart=apart)
                extra = pack(kernel, more, plan, y_blocks)
                plan, extra = lax.optimization_barrier((plan, extra))
                turn = [(i, (i + apart) % rows) for i in range(rows)]
                extra = lax.ppermute(extra, row_axes, turn)
                got[slots] = lax.cond(
                    chosen >= 0, exchange, lambda *_: nothing([room(slots)])[0], plan, y_blocks
                )
            else:
                extra = unused[-1]
                got[slots] = exchange(plan, y_blocks)
            return [extra] + [got[s] for s in SLOTS]

        return branch

    branches = [with_slots(s) for s in SLOTS]
    branches += [with_slots(s, apart) for s in BASES for apart in range(1, rows)]

    got = lax.switch(pick[0], branches, plan, pick[0], y_blocks)

    out = pl.pallas_call(
        functools.partial(product_kernel, targets=targets),
        out_shape=jax.ShapeDtypeStruct((targets,) + block, jnp.float32),
        in_specs=[SMEM] + [HBM] * (3 + len(SLOTS)),
        out_specs=HBM,
        scratch_shapes=[
            pltpu.VMEM((LANES,) + block, jnp.float32),
            pltpu.VMEM((LANES,) + block, jnp.float32),
            pltpu.VMEM((targets + 1,) + block, jnp.float32),
            pltpu.SMEM((LANES + TOGETHER,), jnp.int32),
            pltpu.SemaphoreType.DMA((LANES // TOGETHER,)),
            pltpu.SemaphoreType.DMA,
        ],
        compiler_params=pltpu.CompilerParams(vmem_limit_bytes=60 * 2**20),
        name="products",
    )(plan, x_all, y_blocks, *got)
    return out[None]


def solution(mesh):
    chips = Mesh(mesh.devices.reshape(4, 2, 2, 8, 2), ("x", "y_hi", "y_lo", "z", "core"))
    row, col = ("x", "y_hi"), ("y_lo", "z", "core")
    flat, blocks = P(row, col), P(row, col, None, None)
    return jax.shard_map(
        local,
        mesh=chips,
        in_specs=(blocks, flat, flat, blocks, flat, flat, flat),
        out_specs=blocks,
        check_vma=False,
    )
```

```python
import functools

import jax
import jax.numpy as jnp
from jax import lax
from jax.experimental import pallas as pl
from jax.experimental.pallas import tpu as pltpu
from jax.sharding import Mesh
from jax.sharding import PartitionSpec as P

LANES = 128
SLOTS = (7, 8, 9, 10, 12, 16)
TOGETHER = 8
HBM = pl.BlockSpec(memory_space=pltpu.HBM)
ANY = pl.BlockSpec(memory_space=pl.ANY)
SMEM = pl.BlockSpec(memory_space=pltpu.SMEM)
VMEM = pl.BlockSpec(memory_space=pltpu.VMEM)


X_PLACE, OWNER, SLOT, TARGET, INNER, TOTAL, FIRST = range(7)
ME, PICK, BASE = 126, 127, 125
BASES, EXTRA = (8,), 4


def sheet_kernel(panel, rest, sheet, *, per_cell):
    cols = panel.shape[0]
    got = panel[...].astype(jnp.float32)
    lane = lax.broadcasted_iota(jnp.int32, (LANES, LANES), 1)
    up = lax.broadcasted_iota(jnp.int32, (LANES, LANES), 0)
    cell = lax.broadcasted_iota(jnp.int32, (cols, LANES), 0)
    mine = cell == lax.broadcasted_iota(jnp.int32, (cols, LANES), 1) // per_cell
    lines = []
    for base in (0, per_cell):
        repeated = jnp.dot(
            got,
            (up == base + lane % per_cell).astype(jnp.float32),
            preferred_element_type=jnp.float32,
        )
        lines.append(jnp.sum(jnp.where(mine, repeated, 0.0), axis=0, keepdims=True))
    whole = jnp.concatenate([v.astype(jnp.int32) for v in lines] + [rest[...]], axis=0)
    for r in range(sheet.shape[0]):
        sheet[r] = whole


def plan_kernel(
    info, plan, pick, spread, *, rows, cell_width, per_cell, group, half, targets, panel_rows
):
    shape = (rows, LANES)
    lane = lax.broadcasted_iota(jnp.int32, shape, 1)
    row = lax.broadcasted_iota(jnp.int32, shape, 0)
    x_row, x_col = info[:, 0, :], info[:, 1, :]
    z_code = info[:, 2, :] * cell_width + info[:, 3, :]
    y_col = info[:, 4, :].astype(jnp.float32)
    owner = lane // group
    inner = (lane // per_cell) % (group // per_cell) * cell_width + x_col
    spread[...] = lax.dot_general(
        y_col,
        (row == owner).astype(jnp.float32),
        (((0,), (0,)), ((), ())),
        preferred_element_type=jnp.float32,
    )
    met = jnp.zeros(shape, jnp.float32)
    for k in range(panel_rows):
        met = jnp.where(inner == k, spread[k : k + 1, :], met)
    code = x_row * cell_width + met.astype(jnp.int32)
    target = jnp.full(shape, -1, jnp.int32)
    first = lane
    for s in reversed(range(targets)):
        wanted = z_code[:, s : s + 1]
        target = jnp.where(code == wanted, s, target)
        first = jnp.where(z_code == wanted, s, first)
    used = target >= 0
    key = jnp.where(used, inner, -1 - lane)
    place = lane % group
    repeat = jnp.zeros(shape, jnp.int32)
    for d in range(1, group):
        same = (pltpu.roll(key, d, 1) == key) & (place >= d)
        repeat = jnp.where(same, d, repeat)
    sent = used & (repeat == 0)
    sent_f = sent.astype(jnp.float32)
    up = lax.broadcasted_iota(jnp.int32, (LANES, LANES), 0)
    across = lax.broadcasted_iota(jnp.int32, (LANES, LANES), 1)
    together = (up // group) == (across // group)
    before = (together & (up < across)).astype(jnp.float32)
    slot = jnp.dot(sent_f, before, preferred_element_type=jnp.float32).astype(jnp.int32)
    count = jnp.dot(sent_f, together.astype(jnp.float32), preferred_element_type=jnp.float32)
    held = slot
    for d in range(1, group):
        held = jnp.where(repeat == d, pltpu.roll(slot, d, 1), held)
    me = lax.axis_index("x") * lax.axis_size("y_hi") + lax.axis_index("y_hi")
    side = lax.axis_index("y_lo")

    own_first = (LANES - group * me) % LANES
    mine = lambda v: pltpu.roll(v, own_first, 1)
    sent_slot, sent_row = mine(jnp.where(sent, slot, -1)), mine(inner)
    blocks = jnp.zeros(shape, jnp.int32)
    for t in range(group):
        blocks = jnp.where(lane == sent_slot[:, t : t + 1], sent_row[:, t : t + 1], blocks)
    plan[0] = blocks
    plan[1] = jnp.where(lane == ME, me, mine(count.astype(jnp.int32)))

    def own(v):
        return jnp.sum(jnp.where(row == me, v.astype(jnp.float32), 0.0), axis=0, keepdims=True)

    used_f = used.astype(jnp.float32)
    rank = jnp.dot(used_f, (up < across).astype(jnp.float32), preferred_element_type=jnp.float32)
    chosen = (own(rank).astype(jnp.int32) == up) & (own(used_f) > 0.0)
    p = lane[:1]
    cell = p // per_cell
    facts = jnp.concatenate(
        [
            (
                cell % half * (2 * per_cell)
                + jnp.where(cell // half == side, 0, per_cell)
                + p % per_cell
            ).astype(jnp.float32),
            owner[:1].astype(jnp.float32),
            own(held),
            own(target),
            own(inner),
            jnp.zeros((3, LANES), jnp.float32),
        ]
    )
    listed = lax.dot_general(
        facts,
        chosen.astype(jnp.float32),
        (((1,), (1,)), ((), ())),
        preferred_element_type=jnp.float32,
    )
    total = jnp.sum(own(used_f), axis=1, keepdims=True)
    needed = jnp.where(owner == row, 0, count.astype(jnp.int32))
    most = jnp.max(needed)
    slots = jnp.int32(0)
    for limit in SLOTS[:-1]:
        slots = slots + (most > limit).astype(jnp.int32)
    base, choice = jnp.int32(SLOTS[-1]), slots
    apart = (row - owner + rows) % rows
    for i, few in reversed(list(enumerate(BASES))):
        over = needed > few
        nearest = jnp.min(jnp.where(over, apart, rows))
        only = jnp.max(jnp.where(over, apart, 0)) == nearest
        fits = only & (most <= few + EXTRA)
        slots = jnp.where(fits, SLOTS.index(few), slots)
        base = jnp.where(fits, few, base)
        choice = jnp.where(fits, len(SLOTS) + (rows - 1) * i + nearest - 1, choice)
    pick[0] = choice
    scalars = total.astype(jnp.int32)
    for at, v in ((ME, me), (PICK, slots), (BASE, base)):
        scalars = jnp.where(lane == at, v, scalars)
    scalars = scalars.astype(jnp.float32)
    plan[2] = jnp.where(
        row == TOTAL, scalars, jnp.where(row == FIRST, own(first), listed)
    ).astype(jnp.int32)


def pack_kernel(plan, y_blocks, out, sem, *, rows):
    me, slots = plan[1, 0, ME], out.shape[1]
    started = jnp.int32(0)
    for r in range(rows):
        count = jnp.where(me == r, 0, jnp.minimum(plan[1, r, 0], slots))

        @pl.loop(0, count)
        def _(j):
            pltpu.make_async_copy(y_blocks.at[plan[0, r, j]], out.at[r, j], sem).start()

        started = started + count

    @pl.loop(0, started)
    def _(_):
        pltpu.make_async_copy(y_blocks.at[0], out.at[0, 0], sem).wait()


def pack_extra_kernel(plan, y_blocks, out, sem, *, rows, slots, apart):
    r = (plan[1, 0, ME] + apart) % rows
    count = jnp.clip(plan[1, r, 0] - slots, 0, EXTRA)

    @pl.loop(0, count)
    def _(j):
        pltpu.make_async_copy(y_blocks.at[plan[0, r, slots + j]], out.at[j], sem).start()

    @pl.loop(0, count)
    def _(j):
        pltpu.make_async_copy(y_blocks.at[0], out.at[j], sem).wait()


def nothing_kernel(*out):
    pass


def product_kernel(plan, x_all, y_blocks, extra, *refs, targets):
    got, (out, x_held, y_held, sums, into, in_sem, out_sem) = refs[:-7], refs[-7:]
    base = plan[2, TOTAL, BASE]
    me, pick, total = plan[2, TOTAL, ME], plan[2, TOTAL, PICK], plan[2, TOTAL, 0]

    for i, brought in enumerate(got):

        @pl.when(pick == i)
        def _():
            @pl.loop(0, total)
            def _(n):
                place, owner = plan[2, X_PLACE, n], plan[2, OWNER, n]
                here = owner == me
                sem = in_sem.at[n // TOGETHER]
                pltpu.make_async_copy(x_all.at[place], x_held.at[n], sem).start()

                @pl.when(here)
                def _():
                    pltpu.make_async_copy(
                        y_blocks.at[plan[2, INNER, n]], y_held.at[n], sem
                    ).start()

                slot = plan[2, SLOT, n]

                @pl.when(jnp.logical_not(here) & (slot < base))
                def _():
                    pltpu.make_async_copy(brought.at[owner, slot], y_held.at[n], sem).start()

                @pl.when(jnp.logical_not(here) & (slot >= base))
                def _():
                    pltpu.make_async_copy(extra.at[slot - base], y_held.at[n], sem).start()

                into[n] = plan[2, TARGET, n]

    for j in range(TOGETHER - 1):
        into[total + j] = targets
    sums[...] = jnp.zeros_like(sums)
    dot = functools.partial(jnp.dot, preferred_element_type=jnp.float32)

    @pl.loop(0, (total + TOGETHER - 1) // TOGETHER)
    def _(i):
        n = i * TOGETHER
        for j in range(TOGETHER):

            @pl.when(n + j < total)
            def _():
                pltpu.make_async_copy(x_all.at[0], x_held.at[n + j], in_sem.at[i]).wait()
                pltpu.make_async_copy(y_blocks.at[0], y_held.at[n + j], in_sem.at[i]).wait()

        products = []
        for j in range(TOGETHER):
            x, y = x_held[n + j], y_held[n + j]
            x_hi, y_hi = x.astype(jnp.bfloat16), y.astype(jnp.bfloat16)
            x_lo = (x - x_hi.astype(jnp.float32)).astype(jnp.bfloat16)
            y_lo = (y - y_hi.astype(jnp.float32)).astype(jnp.bfloat16)
            products.append(
                dot(
                    jnp.concatenate([x_hi, x_lo, x_hi], axis=1),
                    jnp.concatenate([y_hi, y_hi, y_lo], axis=0),
                )
            )
        for j in range(TOGETHER):
            sums[into[n + j]] += products[j]

    for s in range(targets):
        pltpu.make_async_copy(sums.at[plan[2, FIRST, s]], out.at[s], out_sem).start()
    for s in range(targets):
        pltpu.make_async_copy(sums.at[0], out.at[s], out_sem).wait()


def local(x_blocks, x_rows, x_cols, y_blocks, y_cols, z_rows, z_cols):
    row_axes, col_axes = ("x", "y_hi"), ("y_lo", "z", "core")
    rows, cols = lax.axis_size(row_axes), lax.axis_size(col_axes)
    x_blocks = x_blocks[0]
    y_blocks = y_blocks[:, 0]
    per_cell, edge = x_blocks.shape[0], x_blocks.shape[-1]
    panel_rows = y_blocks.shape[0]
    targets = z_rows.shape[1]
    group = cols * per_cell // rows
    cell_width = panel_rows * rows // cols
    half = cols // 2
    block = (edge, edge)

    own = jnp.pad(jnp.concatenate([x_rows[0], x_cols[0]]), (0, LANES - 2 * per_cell))
    own = jnp.broadcast_to(own, (cols, 1, LANES))
    rest = jnp.stack(
        [jnp.pad(v, (0, LANES - v.shape[0])) for v in (z_rows[0], z_cols[0], y_cols[:, 0])]
    )
    own, x_blocks = lax.optimization_barrier((own, x_blocks))
    panel = lax.all_to_all(own, col_axes, 0, 0, tiled=True).reshape(cols, LANES)

    across = lax.ppermute(x_blocks, "y_lo", [(0, 1), (1, 0)])
    pair = jnp.concatenate([x_blocks, across], axis=0)
    panel, rest, pair = lax.optimization_barrier((panel, rest, pair))
    x_all = lax.all_gather(pair, ("z", "core"), axis=0, tiled=True)

    sheet = pl.pallas_call(
        functools.partial(sheet_kernel, per_cell=per_cell),
        out_shape=jax.ShapeDtypeStruct((rows, 5, LANES), jnp.int32),
        in_specs=[VMEM] * 2,
        out_specs=VMEM,
        compiler_params=pltpu.CompilerParams(vmem_limit_bytes=4 * 2**20),
        name="sheet",
    )(panel, rest)
    info = lax.all_to_all(sheet, row_axes, 0, 0, tiled=True)

    plan, pick = pl.pallas_call(
        functools.partial(
            plan_kernel,
            rows=rows,
            cell_width=cell_width,
            per_cell=per_cell,
            group=group,
            half=half,
            targets=targets,
            panel_rows=panel_rows,
        ),
        out_shape=(
            jax.ShapeDtypeStruct((3, rows, LANES), jnp.int32),
            jax.ShapeDtypeStruct((1,), jnp.int32),
        ),
        in_specs=[VMEM],
        out_specs=(VMEM, SMEM),
        scratch_shapes=[pltpu.VMEM((LANES, LANES), jnp.float32)],
        compiler_params=pltpu.CompilerParams(vmem_limit_bytes=4 * 2**20),
        name="plan",
    )(info)

    def room(slots):
        return jax.ShapeDtypeStruct((rows, slots) + block, jnp.float32)

    more = jax.ShapeDtypeStruct((EXTRA,) + block, jnp.float32)

    def pack(kernel, shape, plan, y_blocks):
        return pl.pallas_call(
            functools.partial(kernel, rows=rows),
            out_shape=shape,
            in_specs=[SMEM, HBM],
            out_specs=VMEM,
            scratch_shapes=[pltpu.SemaphoreType.DMA],
            compiler_params=pltpu.CompilerParams(vmem_limit_bytes=40 * 2**20),
            name="pack",
        )(plan, y_blocks)

    def nothing(shapes):
        return pl.pallas_call(
            nothing_kernel, out_shape=shapes, out_specs=[HBM] * len(shapes), name="unused"
        )()

    def with_slots(slots, apart=0):
        def exchange(plan, y_blocks):
            packed = pack(pack_kernel, room(slots), plan, y_blocks)
            return lax.all_to_all(packed, row_axes, 0, 0, tiled=True)

        def branch(plan, chosen, y_blocks):
            others = [s for s in SLOTS if s != slots]
            unused = nothing([room(s) for s in others] + [more] * (apart == 0))
            plan, unused = lax.optimization_barrier((plan, unused))
            got = dict(zip(others, unused))
            if apart:
                kernel = functools.partial(pack_extra_kernel, slots=slots, apart=apart)
                extra = pack(kernel, more, plan, y_blocks)
                plan, extra = lax.optimization_barrier((plan, extra))
                turn = [(i, (i + apart) % rows) for i in range(rows)]
                extra = lax.ppermute(extra, row_axes, turn)
                got[slots] = lax.cond(
                    chosen >= 0, exchange, lambda *_: nothing([room(slots)])[0], plan, y_blocks
                )
            else:
                extra = unused[-1]
                got[slots] = exchange(plan, y_blocks)
            return [extra] + [got[s] for s in SLOTS]

        return branch

    branches = [with_slots(s) for s in SLOTS]
    branches += [with_slots(s, apart) for s in BASES for apart in range(1, rows)]

    got = lax.switch(pick[0], branches, plan, pick[0], y_blocks)

    out = pl.pallas_call(
        functools.partial(product_kernel, targets=targets),
        out_shape=jax.ShapeDtypeStruct((targets,) + block, jnp.float32),
        in_specs=[SMEM] + [HBM] * (3 + len(SLOTS)),
        out_specs=HBM,
        scratch_shapes=[
            pltpu.VMEM((LANES,) + block, jnp.float32),
            pltpu.VMEM((LANES,) + block, jnp.float32),
            pltpu.VMEM((targets + 1,) + block, jnp.float32),
            pltpu.SMEM((LANES + TOGETHER,), jnp.int32),
            pltpu.SemaphoreType.DMA((LANES // TOGETHER,)),
            pltpu.SemaphoreType.DMA,
        ],
        compiler_params=pltpu.CompilerParams(vmem_limit_bytes=60 * 2**20),
        name="products",
    )(plan, x_all, y_blocks, *got)
    return out[None]


def solution(mesh):
    chips = Mesh(mesh.devices.reshape(4, 2, 2, 8, 2), ("x", "y_hi", "y_lo", "z", "core"))
    row, col = ("x", "y_hi"), ("y_lo", "z", "core")
    flat, blocks = P(row, col), P(row, col, None, None)
    return jax.shard_map(
        local,
        mesh=chips,
        in_specs=(blocks, flat, flat, blocks, flat, flat, flat),
        out_specs=blocks,
        check_vma=False,
    )
```
